128 devices in a mesh: section: 8 (over y_lo, z), tensor: 16 (over y_hi, x, core).
Axes of the slice: x: 4, y: 4 (y_hi: 2, y_lo: 2; y = y_hi * 2 + y_lo), z: 4, core: 2. Of those that a mesh axis runs over, the one named last changes fastest.
Arguments:
- hidden_state: bfloat16 [64, 8192], P('section'), may hold values from -6 to 6
- norm_gain: float32 [8192], replicated, may hold values from 0.5 to 1.5
- wq_old: bfloat16 [8192, 8192], P('section', 'tensor'), may hold values from -0.0625 to 0.0625
- wkv_old: bfloat16 [8192, 2048], P('tensor', 'section'), may hold values from -0.0625 to 0.0625
- kv_old: bfloat16 [8, 4096, 16, 256], P('section', 'tensor'), may hold values from -241 to 241
- page_table: int32 [64, 64], replicated, may hold values from 0 to 4095, as said below
- lengths: int32 [64], replicated, may hold values from 1 to 1023
Outputs:
- context: bfloat16 [64, 8192], P('section', 'tensor')
- kv_new: bfloat16 [64, 16, 1024, 256], P('section', 'tensor')
- wq_new: bfloat16 [8192, 8192], P(None, 'tensor')
- wkv_new: bfloat16 [8192, 4096], P(None, 'tensor')
The draws below stay inside these ranges and needn't reach their ends.
Inputs may be any that keep to these rules, and one draw needn't show every extreme that they name: `page_table`: every pool page belongs to exactly one page of one request. Each block of 256 consecutive pool pages holds exactly 4 pages of every request.
All inputs are finite; a program needn't handle non-finite values.
Results may differ from the reference program's by a relative error of at most 0.0075.
The reference program's roundings to bfloat16 on the way (of `normed`, `fresh`, `cache` and `probs`) count: a program that leaves them out, or rounds other values in their place, can miss the bound.
Values may be sent and summed in bfloat16 or wider, within the bound.
No kernel may reach another device: no remote copies, remote signals or barrier semaphores. Data moves between devices by JAX's collectives and lax.ppermute only.
A program may use at most 128 MiB of HBM per device.

```python
import jax
import jax.numpy as jnp
from jax import lax

D = 8192
HEADS = 64
KV_HEADS = 8
HEAD_DIM = 128
PAGE = 16
REQS = 64
MAXPAGES = 64
SLOTS = 1024
POOL = 4096
POOL_BLOCKS = 16
KV_COPIES = 16


def draw_page_table(key, part):
    per_block = MAXPAGES // POOL_BLOCKS
    pool_dev = POOL // POOL_BLOCKS
    slot_keys = jax.random.split(jax.random.fold_in(key, 11), REQS)
    orders = jax.vmap(lambda item: jax.random.permutation(item, MAXPAGES))(slot_keys)
    block = orders // per_block
    within = orders % per_block
    block_keys = jax.random.split(jax.random.fold_in(key, 12), POOL_BLOCKS)
    spots = jax.vmap(lambda item: jax.random.permutation(item, pool_dev))(block_keys)
    request = jnp.arange(REQS, dtype=jnp.int32)[:, None]
    local = spots[block, request * per_block + within]
    return (block * pool_dev + local).astype(jnp.int32)


def draw_kv_old(key, part):
    shape = (KV_HEADS, POOL, PAGE, 2 * HEAD_DIM)
    base = jnp.clip(jax.random.normal(jax.random.fold_in(key, 21), shape, jnp.float32), -6.0, 6.0)
    return base.astype(jnp.bfloat16)


def touch_ends(drawn, stream_key, low, top_value):
    shape = drawn.shape
    spot = [jax.random.randint(jax.random.fold_in(stream_key, axis), (), 0, shape[axis]) for axis in range(len(shape))]
    drawn = drawn.at[tuple(spot)].set(low)
    longest = shape.index(max(shape))
    spot[longest] = (spot[longest] + 1) % shape[longest]
    return drawn.at[tuple(spot)].set(top_value)


def shard_levels(own_key, dims, cuts, smallest, top_value):
    gain, own = 1.0, jax.random.fold_in(own_key, 6)
    for dim, shards_of in cuts:
        draws = jnp.exp(jax.random.uniform(jax.random.fold_in(own, dim), (shards_of,), jnp.float32, smallest / len(cuts), top_value / len(cuts)))
        gain = gain * jnp.repeat(draws, dims[dim] // shards_of).reshape([-1 if axis == dim else 1 for axis in range(len(dims))])
    return gain


def centred(own_key, extent, deviation, most, cuts=(), kind=jnp.bfloat16):
    values = jax.random.normal(own_key, extent, jnp.float32) * deviation
    if len(cuts) > 0:
        values = shard_levels(own_key, extent, cuts, -0.22, 0.18) * values
    return jnp.clip(values, min=-most, max=most).astype(kind)


def setup_inputs(seed: int = 0) -> dict:
    key_of = jax.random.split(jax.random.key(seed), 8)
    hidden_state = centred(key_of[0], (REQS, D), 1.0, 6.0, ((0, 8),))
    norm_gain = jnp.clip(1.0 + 0.1 * jax.random.normal(key_of[1], (D,), jnp.float32), 0.5, 1.5)
    wq_old = centred(key_of[2], (D, HEADS * HEAD_DIM), D ** -0.5, 0.0625, ((0, 8), (1, 16)))
    wkv_old = centred(key_of[3], (D, KV_HEADS * 2 * HEAD_DIM), D ** -0.5, 0.0625, ((0, 16), (1, 8)))
    kv_old = draw_kv_old(jax.random.fold_in(key_of[7], 71), 0)
    page_table = draw_page_table(jax.random.fold_in(key_of[7], 71), 0)
    lengths = touch_ends(jax.random.randint(key_of[6], (REQS,), 1, SLOTS), jax.random.fold_in(key_of[6], 1), 1, SLOTS - 1).astype(jnp.int32)
    return {"hidden_state": hidden_state, "norm_gain": norm_gain, "wq_old": wq_old, "wkv_old": wkv_old, "kv_old": kv_old, "page_table": page_table, "lengths": lengths}


EPSILON = 1e-05
ROPE_BASE = 500000.0

def rotate(values, position, head_dim):
    half = head_dim // 2
    frequency = ROPE_BASE ** (-(jnp.arange(half, dtype=jnp.float32) * 2.0 / head_dim))
    angles = position.astype(jnp.float32)[:, None] * frequency[None, :]
    cosine = jnp.cos(angles)[:, None, :]
    sine = jnp.sin(angles)[:, None, :]
    first = values[..., :half]
    second = values[..., half:]
    return jnp.concatenate([first * cosine - second * sine, second * cosine + first * sine], axis=-1)

def reference(hidden_state, norm_gain, wq_old, wkv_old, kv_old, page_table, lengths):
    width = 2 * HEAD_DIM
    group = HEADS // KV_HEADS
    repeats = KV_COPIES // KV_HEADS
    widened = hidden_state.astype(jnp.float32)
    scale = lax.rsqrt(lax.optimization_barrier(jnp.mean(widened * widened, axis=1, keepdims=True)) + EPSILON)
    normed = (widened * scale * norm_gain.astype(jnp.float32)).astype(jnp.bfloat16)
    query = jnp.dot(normed, wq_old, preferred_element_type=jnp.float32).reshape(REQS, HEADS, HEAD_DIM)
    query = rotate(query, lengths, HEAD_DIM).astype(jnp.bfloat16)
    fresh = jnp.dot(normed, wkv_old, preferred_element_type=jnp.float32).reshape(REQS, KV_HEADS, width)
    fresh_key = rotate(fresh[:, :, :HEAD_DIM], lengths, HEAD_DIM)
    fresh = jnp.concatenate([fresh_key, fresh[:, :, HEAD_DIM:]], axis=2).astype(jnp.bfloat16)
    slot_ids = jnp.arange(SLOTS, dtype=jnp.int32)
    written = slot_ids[None, :] == lengths[:, None]
    visible = slot_ids[None, :] <= lengths[:, None]

    def per_head(head):
        pages = kv_old[head][page_table]
        cache = pages.reshape(REQS, SLOTS, width)
        token = lax.dynamic_index_in_dim(fresh, head, 1, keepdims=False)
        cache = jnp.where(written[:, :, None], token[:, None, :], cache)
        queries = lax.dynamic_slice_in_dim(query, head * group, group, 1).astype(jnp.float32)
        scores = jnp.einsum('rgd,rsd->rgs', queries, cache[:, :, :HEAD_DIM].astype(jnp.float32)) * HEAD_DIM ** (-0.5)
        seen = visible[:, None, :]
        peak = lax.optimization_barrier(jnp.max(jnp.where(seen, scores, -jnp.inf), axis=2, keepdims=True))
        weights = jnp.where(seen, jnp.exp(scores - peak), 0.0)
        probs = (weights / lax.optimization_barrier(jnp.sum(weights, axis=2, keepdims=True))).astype(jnp.bfloat16)
        mixed = jnp.einsum('rgs,rsd->rgd', probs.astype(jnp.float32), cache[:, :, HEAD_DIM:].astype(jnp.float32))
        return (cache, mixed.astype(jnp.bfloat16))
    caches, mixed = lax.map(per_head, jnp.arange(KV_HEADS, dtype=jnp.int32))
    context = jnp.moveaxis(mixed, 0, 1).reshape(REQS, HEADS * HEAD_DIM)
    kv_new = jnp.repeat(jnp.moveaxis(caches, 0, 1), repeats, axis=1)
    wkv_new = jnp.repeat(wkv_old.reshape(D, KV_HEADS, width), repeats, axis=1).reshape(D, KV_COPIES * width)
    return (context, kv_new, wq_old, wkv_new)
```

```python
import functools

import jax
import jax.numpy as jnp
from jax import lax
from jax.experimental import pallas as pl
from jax.experimental.pallas import tpu as pltpu
from jax.sharding import Mesh
from jax.sharding import PartitionSpec as P

KV_HEADS = 8
HEAD_DIM = 128
WIDTH = 2 * HEAD_DIM
SECTION = ("yl", "z")
TENSOR = ("yh", "x", "core")
EPSILON = 1e-05
ROPE_BASE = 500000.0
VMEM_LIMIT = 48 * 1024 * 1024

F = 256

ANY = pl.BlockSpec(memory_space=pl.ANY)
VM = pl.BlockSpec(memory_space=pltpu.VMEM)
SM = pl.BlockSpec(memory_space=pltpu.SMEM)


def params():
    return pltpu.CompilerParams(vmem_limit_bytes=VMEM_LIMIT)


def cost(flops, nbytes):
    return pl.CostEstimate(flops=flops, bytes_accessed=nbytes, transcendentals=0)


def shift(value, axis, by):
    n = lax.axis_size(axis)
    return lax.ppermute(value, axis, [(i, (i + by) % n) for i in range(n)])


def pick_kernel(table_ref, kv_ref, out_ref, src_ref, pool, picked, spots, spots_s, sems):
    reqs, width = table_ref.shape
    pages = kv_ref.shape[1]
    per_block = pages // reqs
    load = pltpu.make_async_copy(kv_ref.at[0], pool, sems.at[0])
    load.start()
    table = table_ref[...]
    block = lax.axis_index("yh") * 8 + lax.axis_index("x") * 2 + lax.axis_index("core")
    owner = table // pages
    local = table % pages
    before = lax.broadcasted_iota(jnp.int32, (width, width), 0)
    after = lax.broadcasted_iota(jnp.int32, (width, width), 1)
    tri = (before < after).astype(jnp.float32)
    mine = owner == block
    rank = jnp.dot(mine.astype(jnp.float32), tri, preferred_element_type=jnp.float32)
    lanes = lax.broadcasted_iota(jnp.int32, (reqs, 128), 1)
    chosen = jnp.zeros((reqs, 128), jnp.int32)
    for k in range(per_block):
        hit = jnp.where(mine & (rank == k), local, 0)
        chosen = jnp.where(lanes == k, jnp.sum(hit, axis=1, keepdims=True), chosen)
    spots[...] = chosen
    move = pltpu.make_async_copy(spots, spots_s, sems.at[1])
    move.start()
    rows = src_ref.shape[0]
    first = pl.multiple_of((lax.axis_index("yl") * 4 + lax.axis_index("z")) * rows, rows)
    own = table_ref[pl.ds(first, rows), :] // pages
    ranks = jnp.zeros((rows, width), jnp.float32)
    for t in range(16):
        at = (own == t).astype(jnp.float32)
        ranks += at * jnp.dot(at, tri, preferred_element_type=jnp.float32)
    request = lax.broadcasted_iota(jnp.int32, (rows, width), 0)
    place = ((own % 2) * 8 + own // 2) * rows + request
    src_ref[...] = place * per_block + ranks.astype(jnp.int32)
    move.wait()
    load.wait()
    group = reqs // 8
    outs = []
    for s in range(8):

        def body(i, _, s=s):
            r = s * group + i
            for k in range(per_block):
                picked[r * per_block + k] = pool[spots_s[r, k]]
            return 0

        lax.fori_loop(0, group, body, 0)
        span = pl.ds(s * group * per_block, group * per_block)
        out = pltpu.make_async_copy(picked.at[span], out_ref.at[s], sems.at[2 + s])
        out.start()
        outs.append(out)
    for out in outs:
        out.wait()


def pick(page_table, kv_old):
    pages, page, width = kv_old.shape[1:]
    reqs = page_table.shape[0]
    return pl.pallas_call(
        pick_kernel,
        out_shape=(
            jax.ShapeDtypeStruct((8, pages // 8, page, width), jnp.bfloat16),
            jax.ShapeDtypeStruct((reqs // 8, page_table.shape[1]), jnp.int32),
        ),
        in_specs=[VM, ANY],
        out_specs=(ANY, VM),
        scratch_shapes=[
            pltpu.VMEM((pages, page, width), jnp.bfloat16),
            pltpu.VMEM((pages, page, width), jnp.bfloat16),
            pltpu.VMEM((reqs, 128), jnp.int32),
            pltpu.SMEM((reqs, 128), jnp.int32),
            pltpu.SemaphoreType.DMA((10,)),
        ],
        compiler_params=params(),
        cost_estimate=cost(0, 8 << 20),
    )(page_table, kv_old)


def join_kernel(plan, first, *refs):
    sources = 1 + max(item[0] for item in plan)
    parts = refs[:sources]
    normed_ref = refs[sources]
    rest = refs[sources + 1 :]
    if not first:
        query_in = rest[0]
        rest = rest[2:]
    whole_ref, query_ref = rest[:2]
    buffers = rest[2 : 2 + sources]
    sem_in, sem_out = rest[2 + sources :]
    yl, z = lax.axis_index("yl"), lax.axis_index("z")
    loads = []
    for i in range(sources):
        load = pltpu.make_async_copy(parts[i], buffers[i], sem_in.at[i])
        load.start()
        loads.append(load)
    total = jnp.zeros(query_ref.shape, jnp.float32) if first else query_in[...]
    outs = []
    waited = set()
    for n, (i, low, rows, dy, dz, at) in enumerate(plan):
        if i not in waited:
            loads[i].wait()
            waited.add(i)
        block = lax.rem(yl + dy, 2) * 4 + lax.rem(z + dz + 4, 4)
        start = pl.multiple_of(block * 1024 + at, 128)
        out = pltpu.make_async_copy(
            buffers[i].at[pl.ds(low, rows)], whole_ref.at[pl.ds(start, rows)], sem_out.at[n]
        )
        out.start()
        outs.append(out)
        total += jnp.dot(
            normed_ref[:, pl.ds(start, rows)],
            buffers[i][low : low + rows, :],
            preferred_element_type=jnp.float32,
        )
    query_ref[...] = total
    for out in outs:
        out.wait()


def join(plan, parts, normed, state=None):
    first = state is None
    columns = parts[0].shape[1]
    rows = normed.shape[0]
    args = [*parts, normed]
    in_specs = [ANY] * len(parts) + [VM]
    aliases = {}
    if not first:
        whole, query = state
        args += [query, whole]
        in_specs += [VM, ANY]
        aliases = {len(parts) + 2: 0}
    nbytes = sum(part.size * 4 for part in parts)
    return pl.pallas_call(
        functools.partial(join_kernel, plan, first),
        out_shape=(
            jax.ShapeDtypeStruct((normed.shape[1], columns), jnp.bfloat16),
            jax.ShapeDtypeStruct((rows, columns), jnp.float32),
        ),
        in_specs=in_specs,
        out_specs=(ANY, VM),
        input_output_aliases=aliases,
        scratch_shapes=[pltpu.VMEM(part.shape, jnp.bfloat16) for part in parts]
        + [pltpu.SemaphoreType.DMA((len(parts),)), pltpu.SemaphoreType.DMA((len(plan),))],
        compiler_params=params(),
        cost_estimate=cost(nbytes * 4, nbytes),
    )(*args)


def order_kernel(src_ref, lengths_ref, fresh_ref, mine_ref, other_ref, out_ref, held, built, sems):
    rows, slots = built.shape[:2]
    page = held.shape[1]
    half = held.shape[0] // 2
    core = lax.axis_index("core")
    here = pl.ds(pl.multiple_of(core * half, half), half)
    there = pl.ds(pl.multiple_of((1 - core) * half, half), half)
    loads = [
        pltpu.make_async_copy(mine_ref, held.at[here], sems.at[0]),
        pltpu.make_async_copy(other_ref, held.at[there], sems.at[1]),
    ]
    for load in loads:
        load.start()
    for load in loads:
        load.wait()
    first = (lax.axis_index("yl") * 4 + lax.axis_index("z")) * rows
    outs = []
    for r in range(rows):

        def body(j, _, r=r):
            for n in range(4):
                at = pl.multiple_of((j * 4 + n) * page, page)
                built[r, pl.ds(at, page), :] = held[src_ref[r, j * 4 + n]]
            return 0

        lax.fori_loop(0, slots // page // 4, body, 0)
        length = lengths_ref[first + r]
        at = pl.multiple_of(length // page * page, page)
        old = built[r, pl.ds(at, page), :]
        line = lax.broadcasted_iota(jnp.int32, old.shape, 0)
        new = jnp.broadcast_to(fresh_ref[r : r + 1, :], old.shape)
        built[r, pl.ds(at, page), :] = jnp.where(
            line == length % page, new, old.astype(jnp.float32)
        ).astype(jnp.bfloat16)
        out = pltpu.make_async_copy(built.at[r], out_ref.at[r, 0], sems.at[2 + r])
        out.start()
        outs.append(out)
    for out in outs:
        out.wait()


def order(src, lengths, fresh, mine, other, rows, slots):
    pages, page, width = mine.shape
    return pl.pallas_call(
        order_kernel,
        out_shape=jax.ShapeDtypeStruct((rows, 1, slots, width), jnp.bfloat16),
        in_specs=[SM, SM, VM, ANY, ANY],
        out_specs=ANY,
        scratch_shapes=[
            pltpu.VMEM((2 * pages, page, width), jnp.bfloat16),
            pltpu.VMEM((rows, slots, width), jnp.bfloat16),
            pltpu.SemaphoreType.DMA((2 + rows,)),
        ],
        compiler_params=params(),
        cost_estimate=cost(0, 16 << 20),
    )(src, lengths, fresh, mine, other)


def attend_kernel(lengths_ref, query_ref, cos_ref, sin_ref, cache_ref, out_ref, cache, heads, mixed, sems):
    rows, slots = cache.shape[:2]
    loads = []
    for r in range(rows):
        load = pltpu.make_async_copy(cache_ref.at[r, 0], cache.at[r], sems.at[r])
        load.start()
        loads.append(load)
    count = query_ref.shape[1] // HEAD_DIM
    heads[...] = jnp.zeros_like(heads)
    for h in range(count):
        value = query_ref[:, h * HEAD_DIM : (h + 1) * HEAD_DIM]
        turned = value * cos_ref[...] + pltpu.roll(value, HEAD_DIM // 2, 1) * sin_ref[...]
        heads[:, h, :] = turned
    first = (lax.axis_index("yl") * 4 + lax.axis_index("z")) * rows
    for r in range(rows):
        loads[r].wait()
        scores = lax.dot_general(
            heads[r].astype(jnp.bfloat16),
            cache[r, :, :HEAD_DIM],
            (((1,), (1,)), ((), ())),
            preferred_element_type=jnp.float32,
        ) * HEAD_DIM ** (-0.5)
        slot = lax.broadcasted_iota(jnp.int32, scores.shape, 1)
        seen = slot <= lengths_ref[first + r]
        peak = jnp.max(jnp.where(seen, scores, -jnp.inf), axis=1, keepdims=True)
        weights = jnp.where(seen, jnp.exp(scores - peak), 0.0)
        probs = (weights / jnp.sum(weights, axis=1, keepdims=True)).astype(jnp.bfloat16)
        result = jnp.dot(probs, cache[r, :, HEAD_DIM:], preferred_element_type=jnp.float32)
        for h in range(count):
            mixed[r : r + 1, h * HEAD_DIM : (h + 1) * HEAD_DIM] = result[h : h + 1, :]
    out_ref[...] = mixed[...].astype(jnp.bfloat16)


def attend(lengths, query, cosine, sine, cache):
    rows, _, slots, width = cache.shape
    return pl.pallas_call(
        attend_kernel,
        out_shape=jax.ShapeDtypeStruct(query.shape, jnp.bfloat16),
        in_specs=[SM, VM, VM, VM, ANY],
        out_specs=VM,
        scratch_shapes=[
            pltpu.VMEM((rows, slots, width), jnp.bfloat16),
            pltpu.VMEM((rows, 8, HEAD_DIM), jnp.float32),
            pltpu.VMEM(query.shape, jnp.float32),
            pltpu.SemaphoreType.DMA((rows,)),
        ],
        compiler_params=params(),
        cost_estimate=cost(64 << 20, 4 << 20),
    )(lengths, query, cosine, sine, cache)


def shards(hidden_state, norm_gain, wq_old, wkv_old, kv_old, page_table, lengths):
    rows = hidden_state.shape[0]
    page = kv_old.shape[2]
    slots = page_table.shape[1] * page
    section_id = lax.axis_index(SECTION)

    up = shift(wq_old, "z", 1)
    down = shift(wq_old, "z", -1)
    across = shift(wq_old, "yl", 1)

    pairs = []
    for yl in range(2):
        for z in range(4):
            for yh in range(2):
                for x in range(4):
                    here = ((yl * 4 + z) * 2 + yh) * 4 + x
                    there = ((yh * 4 + x) * 2 + yl) * 4 + z
                    pairs.append((here, there))
    turned = lax.ppermute(wkv_old, ("yl", "z", "yh", "x"), pairs)
    wkv_new = lax.all_gather(turned, ("yl", "z", "core"), axis=0, tiled=True)

    picked, src = pick(page_table, kv_old)
    by_head = lax.all_to_all(picked, SECTION, split_axis=0, concat_axis=0, tiled=True)
    mine = lax.all_to_all(by_head, ("yh", "x"), split_axis=0, concat_axis=0, tiled=True)
    mine = mine.reshape(-1, page, WIDTH)
    other = shift(mine, "core", 1)

    half = wq_old.shape[0] // 2
    rest = wq_old.shape[0] - F
    to_up = jnp.concatenate([up[:half], across[F:]])
    to_down = jnp.concatenate([down[half:], across[F:]])
    to_across = jnp.concatenate([up[:F], down[:F]])
    up2 = shift(to_up, "z", 1)
    down2 = shift(to_down, "z", -1)
    across2 = shift(to_across, "yl", 1)

    split = rest // 2
    up3 = shift(up2[half : half + split], "z", 1)
    down3 = shift(down2[half + split :], "z", -1)
    across3 = shift(up2[:F], "yl", 1)

    widened = hidden_state.astype(jnp.float32)
    scale = lax.rsqrt(jnp.mean(widened * widened, axis=1, keepdims=True) + EPSILON)
    normed = (widened * scale * norm_gain[None, :]).astype(jnp.bfloat16)

    state = join(
        ((0, 0, 1024, 0, 0, 0), (1, 0, 1024, 0, -1, 0), (2, 0, 1024, 0, 1, 0), (3, 0, 1024, 1, 0, 0)),
        (wq_old, up, down, across),
        normed,
    )
    state = join(
        (
            (0, 0, half, 0, 2, 0),
            (0, half, rest, 1, -1, F),
            (1, 0, half, 0, 2, half),
            (1, half, rest, 1, 1, F),
            (2, 0, F, 1, -1, 0),
            (2, F, F, 1, 1, 0),
        ),
        (up2, down2, across2),
        normed,
        state,
    )
    wq_new, query = join(
        ((0, 0, split, 1, 2, F), (1, 0, split, 1, 2, F + split), (2, 0, F, 1, 2, 0)),
        (up3, down3, across3),
        normed,
        state,
    )

    my_lengths = lax.dynamic_slice_in_dim(lengths, section_id * rows, rows, 0)
    spread = HEAD_DIM // 2
    frequency = ROPE_BASE ** (-(jnp.arange(spread, dtype=jnp.float32) * 2.0 / HEAD_DIM))
    angles = my_lengths.astype(jnp.float32)[:, None] * frequency[None, :]
    cosine, sine = jnp.cos(angles), jnp.sin(angles)
    cosine = jnp.concatenate([cosine, cosine], axis=1)
    sine = jnp.concatenate([-sine, sine], axis=1)

    fresh = jnp.dot(normed, wkv_new, preferred_element_type=jnp.float32)
    key = fresh[:, :HEAD_DIM]
    key = key * cosine + jnp.concatenate([key[:, spread:], key[:, :spread]], axis=1) * sine
    fresh = jnp.concatenate([key, fresh[:, HEAD_DIM:]], axis=1)
    kv_new = order(src, lengths, fresh, mine, other, rows, slots)
    context = attend(lengths, query, cosine, sine, kv_new)
    return (context, kv_new, wq_new, wkv_new)


def solution(mesh):
    torus = Mesh(mesh.devices.reshape(2, 4, 2, 4, 2), ("yl", "z", "yh", "x", "core"))
    return jax.shard_map(
        shards,
        mesh=torus,
        in_specs=(
            P(SECTION, None),
            P(),
            P(SECTION, TENSOR),
            P(TENSOR, SECTION),
            P(SECTION, TENSOR, None, None),
            P(),
            P(),
        ),
        out_specs=(
            P(SECTION, TENSOR),
            P(SECTION, TENSOR, None, None),
            P(None, TENSOR),
            P(None, TENSOR),
        ),
        check_vma=False,
    )
```

```python
import functools

import jax
import jax.numpy as jnp
from jax import lax
from jax.experimental import pallas as pl
from jax.experimental.pallas import tpu as pltpu
from jax.sharding import Mesh
from jax.sharding import PartitionSpec as P

KV_HEADS = 8
HEAD_DIM = 128
WIDTH = 2 * HEAD_DIM
SECTION = ("yl", "z")
TENSOR = ("yh", "x", "core")
EPSILON = 1e-05
ROPE_BASE = 500000.0
VMEM_LIMIT = 48 * 1024 * 1024

F = 256

ANY = pl.BlockSpec(memory_space=pl.ANY)
HBM = pl.BlockSpec(memory_space=pltpu.HBM)
VM = pl.BlockSpec(memory_space=pltpu.VMEM)
SM = pl.BlockSpec(memory_space=pltpu.SMEM)


def params():
    return pltpu.CompilerParams(vmem_limit_bytes=VMEM_LIMIT)


def cost(flops, nbytes):
    return pl.CostEstimate(flops=flops, bytes_accessed=nbytes, transcendentals=0)


def block_of(dy, dz):
    return lax.rem(lax.axis_index("yl") + dy, 2) * 4 + lax.rem(lax.axis_index("z") + dz + 4, 4)


def source_of(dy, dz):
    gap = lax.axis_index("z") + dz - lax.axis_index("x") + 8
    return lax.rem(lax.axis_index("yl") + dy, 2) * 4 + lax.rem(gap, 4)


def shift(value, axis, by):
    n = lax.axis_size(axis)
    return lax.ppermute(value, axis, [(i, (i + by) % n) for i in range(n)])


def pick_kernel(table_ref, kv_ref, *refs):
    out_refs, src_ref = refs[:2], refs[2]
    pool, picked, spots, spots_s, sems = refs[3:]
    reqs, width = table_ref.shape
    pages = kv_ref.shape[1]
    per_block = pages // reqs
    load = pltpu.make_async_copy(kv_ref.at[0], pool, sems.at[0])
    load.start()
    yl, z = lax.axis_index("yl"), lax.axis_index("z")
    yh, x, core = lax.axis_index("yh"), lax.axis_index("x"), lax.axis_index("core")
    table = table_ref[...]
    owner = table // pages
    local = table % pages
    before = lax.broadcasted_iota(jnp.int32, (width, width), 0)
    after = lax.broadcasted_iota(jnp.int32, (width, width), 1)
    tri = (before < after).astype(jnp.float32)
    mine = owner == yh * 8 + x * 2 + core
    rank = jnp.dot(mine.astype(jnp.float32), tri, preferred_element_type=jnp.float32)
    lanes = lax.broadcasted_iota(jnp.int32, (reqs, 128), 1)
    chosen = jnp.zeros((reqs, 128), jnp.int32)
    for k in range(per_block):
        hit = jnp.where(mine & (rank == k), local, 0)
        chosen = jnp.where(lanes == k, jnp.sum(hit, axis=1, keepdims=True), chosen)
    spots[...] = chosen
    move = pltpu.make_async_copy(spots, spots_s, sems.at[1])
    move.start()
    rows = src_ref.shape[0]
    first = pl.multiple_of((yl * 4 + z) * rows, rows)
    own = table_ref[pl.ds(first, rows), :] // pages
    ranks = jnp.zeros((rows, width), jnp.float32)
    for t in range(16):
        at = (own == t).astype(jnp.float32)
        ranks += at * jnp.dot(at, tri, preferred_element_type=jnp.float32)
    request = lax.broadcasted_iota(jnp.int32, (rows, width), 0)
    place = (own + core) % 2 * 4 + (x + 4 - own // 2 % 4) % 4
    place = place * 2 + (own // 8 + yl) % 2
    place = (place * rows + request) * per_block
    src_ref[...] = place + ranks.astype(jnp.int32)
    move.wait()
    load.wait()
    outs = []
    for n in range(8):
        turn, dz = n // 4, n % 4
        start = (lax.rem(yh + turn, 2) * 4 + lax.rem(z + dz, 4)) * rows

        def body(i, _, n=n, start=start):
            for k in range(per_block):
                picked[(n * rows + i) * per_block + k] = pool[spots_s[start + i, k]]
            return 0

        lax.fori_loop(0, rows, body, 0)
        size = rows * per_block
        out = pltpu.make_async_copy(
            picked.at[pl.ds(n * size, size)],
            out_refs[turn].at[pl.ds(dz * size, size)],
            sems.at[2 + n],
        )
        out.start()
        outs.append(out)
    for out in outs:
        out.wait()


def pick(page_table, kv_old):
    pages, page, width = kv_old.shape[1:]
    reqs = page_table.shape[0]
    part = jax.ShapeDtypeStruct((pages // 2, page, width), jnp.bfloat16)
    return pl.pallas_call(
        pick_kernel,
        out_shape=(part, part, jax.ShapeDtypeStruct((reqs // 8, page_table.shape[1]), jnp.int32)),
        in_specs=[VM, ANY],
        out_specs=(ANY, ANY, VM),
        scratch_shapes=[
            pltpu.VMEM((pages, page, width), jnp.bfloat16),
            pltpu.VMEM((pages, page, width), jnp.bfloat16),
            pltpu.VMEM((reqs, 128), jnp.int32),
            pltpu.SMEM((reqs, 128), jnp.int32),
            pltpu.SemaphoreType.DMA((10,)),
        ],
        compiler_params=params(),
        cost_estimate=cost(0, 4 << 20),
    )(page_table, kv_old)


def staged_kernel(copies, sources, size, *refs):
    parts, out, stage, sems = refs[:sources], refs[-3], refs[-2], refs[-1]
    moves = []
    for n, (i, low, col, rows, _, at) in enumerate(copies):
        move = pltpu.make_async_copy(
            parts[i].at[pl.ds(low, rows), pl.ds(col, WIDTH)], stage.at[pl.ds(at, rows)], sems.at[n, 0]
        )
        move.start()
        moves.append(move)
    outs = []
    for n, (i, low, col, rows, _, at) in enumerate(copies):
        moves[n].wait()
        span = pl.ds(at, rows)
        move = pltpu.make_async_copy(stage.at[span], out.at[span], sems.at[n, 1])
        move.start()
        outs.append(move)
    for move in outs:
        move.wait()


def staged(layout, parts, after=()):
    copies, at = [], 0
    for i, low, col, rows in layout:
        copies.append((i, low, col, rows, 0, at))
        at += rows
    return pl.pallas_call(
        functools.partial(staged_kernel, tuple(copies), len(parts), at),
        out_shape=jax.ShapeDtypeStruct((at, WIDTH), jnp.bfloat16),
        in_specs=[ANY] * (len(parts) + len(after)),
        out_specs=ANY,
        scratch_shapes=[
            pltpu.VMEM((at, WIDTH), jnp.bfloat16),
            pltpu.SemaphoreType.DMA((len(copies), 2)),
        ],
        compiler_params=params(),
        cost_estimate=cost(0, at * WIDTH * 4),
    )(*parts, *after)


def pack_kernel(copies, sources, sizes, *refs):
    parts, outs, sems = refs[:sources], refs[-1 - len(sizes) : -1], refs[-1]
    moves = []
    for n, (i, low, col, rows, o, at) in enumerate(copies):
        move = pltpu.make_async_copy(
            parts[i].at[pl.ds(low, rows), pl.ds(col, WIDTH)],
            outs[o].at[pl.ds(at, rows)],
            sems.at[n],
        )
        move.start()
        moves.append(move)
    for move in moves:
        move.wait()


def pack(layouts, parts, after=()):
    copies, sizes = [], []
    for o, layout in enumerate(layouts):
        at = 0
        for i, low, col, rows in layout:
            copies.append((i, low, col, rows, o, at))
            at += rows
        sizes.append(at)
    return pl.pallas_call(
        functools.partial(pack_kernel, tuple(copies), len(parts), tuple(sizes)),
        out_shape=[jax.ShapeDtypeStruct((size, WIDTH), jnp.bfloat16) for size in sizes],
        in_specs=[ANY] * (len(parts) + len(after)),
        out_specs=[ANY] * len(sizes),
        scratch_shapes=[pltpu.SemaphoreType.DMA((len(copies),))],
        compiler_params=params(),
        cost_estimate=cost(0, sum(sizes) * WIDTH * 4),
    )(*parts, *after)


def sort_kernel(parts, lows, count, *refs):
    ins, outs = refs[:parts], refs[-6:-2]
    held, sems = refs[-2:]
    moves = []
    for n, (i, low, dz, at) in enumerate(lows):
        move = pltpu.make_async_copy(
            ins[i].at[pl.ds(low, count)], held.at[dz, pl.ds(at, count)], sems.at[n]
        )
        move.start()
        moves.append(move)
    for move in moves:
        move.wait()
    gap = lax.axis_index("z") - lax.axis_index("x") + 8
    moves = []
    for dx in range(4):
        move = pltpu.make_async_copy(held.at[lax.rem(gap - dx, 4)], outs[dx], sems.at[dx])
        move.start()
        moves.append(move)
    for move in moves:
        move.wait()


def sort(parts, lows, count, after=()):
    return pl.pallas_call(
        functools.partial(sort_kernel, len(parts), tuple(lows), count),
        out_shape=[jax.ShapeDtypeStruct((2 * count, WIDTH), jnp.bfloat16)] * 4,
        in_specs=[ANY] * (len(parts) + len(after)),
        out_specs=[ANY] * 4,
        scratch_shapes=[
            pltpu.VMEM((4, 2 * count, WIDTH), jnp.bfloat16),
            pltpu.SemaphoreType.DMA((len(lows),)),
        ],
        compiler_params=params(),
        cost_estimate=cost(0, 8 << 20),
    )(*parts, *after)


def land(plan, buffers, loads, wholes, normed_ref, query, fresh, sems):
    outs, waited = [], set()
    query = list(query)
    for n, (i, low, rows, kind, dy, dz, at, col, width) in enumerate(plan):
        if i not in waited:
            loads[i].wait()
            waited.add(i)
        if kind == "q":
            start = pl.multiple_of(block_of(dy, dz) * 1024 + at, 128)
            whole = wholes[0].at[pl.ds(start, rows), pl.ds(col, width)]
        else:
            core = lax.axis_index("core")
            half = core if kind == "own" else 1 - core
            start = pl.multiple_of((source_of(dy, dz) * 2 + half) * 512, 512)
            whole = wholes[1].at[pl.ds(start, rows)]
        out = pltpu.make_async_copy(buffers[i].at[pl.ds(low, rows)], whole, sems.at[n])
        out.start()
        outs.append(out)
        normed = normed_ref[:, pl.ds(start, rows)]
        for c in range(0, width, WIDTH):
            term = jnp.dot(
                normed,
                buffers[i][low : low + rows, c : c + WIDTH],
                preferred_element_type=jnp.float32,
            )
            if kind == "q":
                query[(col + c) // WIDTH] += term
            else:
                fresh += term
    return query, fresh, outs


def join_kernel(plan, count, state, *refs):
    parts, normed_ref = refs[:count], refs[count]
    rest = refs[count + 1 :]
    wholes_n = 2 if any(item[3] != "q" for item in plan) else 1
    rows, columns = normed_ref.shape[0], 2 * WIDTH
    if state:
        query_in, rest = rest[0], rest[2:]
        query = [query_in[:, :WIDTH], query_in[:, WIDTH:]]
    else:
        query = [jnp.zeros((rows, WIDTH), jnp.float32)] * 2
    wholes, rest = rest[:wholes_n], rest[wholes_n:]
    query_ref, rest = rest[0], rest[1:]
    if wholes_n == 2:
        fresh_ref, rest = rest[0], rest[1:]
    buffers, sem_in, sem_out = rest[:count], rest[count], rest[count + 1]
    loads = []
    for i in range(count):
        load = pltpu.make_async_copy(parts[i], buffers[i], sem_in.at[i])
        load.start()
        loads.append(load)
    fresh = jnp.zeros((rows, WIDTH), jnp.float32)
    query, fresh, outs = land(plan, buffers, loads, wholes, normed_ref, query, fresh, sem_out)
    query_ref[:, :WIDTH] = query[0]
    query_ref[:, WIDTH:] = query[1]
    if wholes_n == 2:
        fresh_ref[...] = fresh
    for out in outs:
        out.wait()


def join(plan, parts, normed, state=None):
    rows, depth = normed.shape
    kv = any(item[3] != "q" for item in plan)
    args = [*parts, normed]
    in_specs = [ANY] * len(parts) + [VM]
    aliases = {}
    if state is not None:
        whole, query = state
        args += [query, whole]
        in_specs += [VM, HBM]
        aliases = {len(parts) + 2: 0}
    out_shape = [jax.ShapeDtypeStruct((depth, 2 * WIDTH), jnp.bfloat16)]
    out_specs = [HBM]
    if kv:
        out_shape.append(jax.ShapeDtypeStruct((depth, WIDTH), jnp.bfloat16))
        out_specs.append(HBM)
    out_shape.append(jax.ShapeDtypeStruct((rows, 2 * WIDTH), jnp.float32))
    out_specs.append(VM)
    if kv:
        out_shape.append(jax.ShapeDtypeStruct((rows, WIDTH), jnp.float32))
        out_specs.append(VM)
    nbytes = sum(part.size * 4 for part in parts)
    return pl.pallas_call(
        functools.partial(join_kernel, plan, len(parts), state is not None),
        out_shape=out_shape,
        in_specs=in_specs,
        out_specs=out_specs,
        input_output_aliases=aliases,
        scratch_shapes=[pltpu.VMEM(part.shape, jnp.bfloat16) for part in parts]
        + [pltpu.SemaphoreType.DMA((len(parts),)), pltpu.SemaphoreType.DMA((len(plan),))],
        compiler_params=params(),
        cost_estimate=cost(0, nbytes),
    )(*args)


def turn(value, cosine, sine):
    return value * cosine + pltpu.roll(value, HEAD_DIM // 2, 1) * sine


def last_kernel(plan, count, pages, page, *refs):
    parts, pools = refs[:count], refs[count : count + len(pages)]
    rest = refs[count + len(pages) :]
    src_ref, lengths_ref, normed_ref, cos_ref, sin_ref, query_ref, fresh_ref = rest[:7]
    rest = rest[9:]
    wq_ref, wkv_ref, cache_ref, context_ref = rest[:4]
    rest = rest[4:]
    buffers, rest = rest[:count], rest[count:]
    held, built, heads, mixed, sem_in, sem_pool, sem_out, sem_cache = rest
    rows, slots = built.shape[:2]
    fills = []
    for n, (i, low, size, at) in enumerate(pages):
        fill = pltpu.make_async_copy(
            pools[n].at[pl.ds(low, size)], held.at[pl.ds(at, size)], sem_pool.at[n]
        )
        fill.start()
        fills.append(fill)
    loads = []
    for i in range(count):
        load = pltpu.make_async_copy(parts[i], buffers[i], sem_in.at[i])
        load.start()
        loads.append(load)
    query = [query_ref[:, :WIDTH], query_ref[:, WIDTH:]]
    query, fresh, outs = land(
        plan, buffers, loads, (wq_ref, wkv_ref), normed_ref, query, fresh_ref[...], sem_out
    )
    cosine, sine = cos_ref[...], sin_ref[...]
    fresh = jnp.concatenate(
        [turn(fresh[:, :HEAD_DIM], cosine, sine), fresh[:, HEAD_DIM:]], axis=1
    )
    count_q = 2 * WIDTH // HEAD_DIM
    heads[...] = jnp.zeros_like(heads)
    for h in range(count_q):
        value = query[h * HEAD_DIM // WIDTH]
        low = h * HEAD_DIM % WIDTH
        heads[:, h, :] = turn(value[:, low : low + HEAD_DIM], cosine, sine)
    for fill in fills:
        fill.wait()
    first = (lax.axis_index("yl") * 4 + lax.axis_index("z")) * rows
    for r in range(rows):

        def body(j, _, r=r):
            for n in range(8):
                at = pl.multiple_of((j * 8 + n) * page, page)
                low = pl.multiple_of(src_ref[r, j * 8 + n] * page, page)
                built[r, pl.ds(at, page), :] = held[pl.ds(low, page), :]
            return 0

        lax.fori_loop(0, slots // page // 8, body, 0)
        length = lengths_ref[first + r]
        at = pl.multiple_of(length // page * page, page)
        old = built[r, pl.ds(at, page), :]
        line = lax.broadcasted_iota(jnp.int32, old.shape, 0)
        new = jnp.broadcast_to(fresh[r : r + 1, :], old.shape)
        built[r, pl.ds(at, page), :] = jnp.where(
            line == length % page, new, old.astype(jnp.float32)
        ).astype(jnp.bfloat16)
        out = pltpu.make_async_copy(built.at[r], cache_ref.at[r, 0], sem_cache.at[r])
        out.start()
        outs.append(out)
    for r in range(rows):
        length = lengths_ref[first + r]
        scores = lax.dot_general(
            heads[r].astype(jnp.bfloat16),
            built[r, :, :HEAD_DIM],
            (((1,), (1,)), ((), ())),
            preferred_element_type=jnp.float32,
        ) * HEAD_DIM ** (-0.5)
        seen = lax.broadcasted_iota(jnp.int32, scores.shape, 1) <= length
        peak = jnp.max(jnp.where(seen, scores, -jnp.inf), axis=1, keepdims=True)
        weights = jnp.where(seen, jnp.exp(scores - peak), 0.0)
        probs = (weights / jnp.sum(weights, axis=1, keepdims=True)).astype(jnp.bfloat16)
        result = jnp.dot(probs, built[r, :, HEAD_DIM:], preferred_element_type=jnp.float32)
        for h in range(count_q):
            mixed[r : r + 1, h * HEAD_DIM : (h + 1) * HEAD_DIM] = result[h : h + 1, :]
    context_ref[...] = mixed[...].astype(jnp.bfloat16)
    for out in outs:
        out.wait()


def last(plan, parts, pages, pools, page, src, lengths, normed, cosine, sine, query, fresh, wq_new, wkv_new):
    rows = normed.shape[0]
    slots = src.shape[1] * page
    pools = [pools[item[0]] for item in pages]
    args = [*parts, *pools, src, lengths, normed, cosine, sine, query, fresh, wq_new, wkv_new]
    lead = len(parts) + len(pools)
    return pl.pallas_call(
        functools.partial(last_kernel, plan, len(parts), tuple(pages), page),
        out_shape=[
            jax.ShapeDtypeStruct(wq_new.shape, jnp.bfloat16),
            jax.ShapeDtypeStruct(wkv_new.shape, jnp.bfloat16),
            jax.ShapeDtypeStruct((rows, 1, slots, WIDTH), jnp.bfloat16),
            jax.ShapeDtypeStruct(query.shape, jnp.bfloat16),
        ],
        in_specs=[ANY] * lead + [SM, SM, VM, VM, VM, VM, VM, HBM, HBM],
        out_specs=[HBM, HBM, HBM, VM],
        input_output_aliases={lead + 7: 0, lead + 8: 1},
        scratch_shapes=[pltpu.VMEM(part.shape, jnp.bfloat16) for part in parts]
        + [
            pltpu.VMEM((rows * slots, WIDTH), jnp.bfloat16),
            pltpu.VMEM((rows, slots, WIDTH), jnp.bfloat16),
            pltpu.VMEM((rows, 8, HEAD_DIM), jnp.float32),
            pltpu.VMEM(query.shape, jnp.float32),
            pltpu.SemaphoreType.DMA((len(parts),)),
            pltpu.SemaphoreType.DMA((len(pages),)),
            pltpu.SemaphoreType.DMA((len(plan),)),
            pltpu.SemaphoreType.DMA((rows,)),
        ],
        compiler_params=params(),
        cost_estimate=cost(64 << 20, 16 << 20),
    )(*args)


def halves(part, low, rows):
    return [(part, low, 0, rows), (part, low, WIDTH, rows)]


def shards(hidden_state, norm_gain, wq_old, wkv_old, kv_old, page_table, lengths):
    rows = hidden_state.shape[0]
    page = kv_old.shape[2]
    half = wq_old.shape[0] // 2
    rest = wq_old.shape[0] - F
    split = rest // 2

    pairs = []
    for yl in range(2):
        for z in range(4):
            for yh in range(2):
                for x in range(4):
                    here = ((yl * 4 + z) * 2 + yh) * 4 + x
                    pairs.append((here, ((yh * 4 + (z + x) % 4) * 2 + yl) * 4 + x))
    turned = lax.ppermute(wkv_old, ("yl", "z", "yh", "x"), pairs)
    turned = lax.ppermute(
        turned, ("z", "x"), [(z * 4 + x, z * 4 + (z - x) % 4) for z in range(4) for x in range(4)]
    )
    up = shift(wq_old, "z", 1)
    down = shift(wq_old, "z", -1)
    picked = pick(page_table, kv_old)
    src = picked[2]
    near, far = [
        lax.ppermute(
            picked[flip].reshape(-1, WIDTH),
            ("yl", "yh"),
            [(a * 2 + b, (b ^ flip) * 2 + a) for a in range(2) for b in range(2)],
        )
        for flip in range(2)
    ]
    across = shift(wq_old, "yl", 1)

    my_lengths = lax.dynamic_slice_in_dim(lengths, lax.axis_index(SECTION) * rows, rows, 0)
    widened = hidden_state.astype(jnp.float32)
    scale = lax.rsqrt(jnp.mean(widened * widened, axis=1, keepdims=True) + EPSILON)
    normed = (widened * scale * norm_gain[None, :]).astype(jnp.bfloat16)
    spread = HEAD_DIM // 2
    frequency = ROPE_BASE ** (-(jnp.arange(spread, dtype=jnp.float32) * 2.0 / HEAD_DIM))
    angles = my_lengths.astype(jnp.float32)[:, None] * frequency[None, :]
    cosine, sine = jnp.cos(angles), jnp.sin(angles)
    cosine = jnp.concatenate([cosine, cosine], axis=1)
    sine = jnp.concatenate([-sine, sine], axis=1)

    chunk = near.shape[0] // 4
    block = turned.shape[0]
    parts = (up, down, near, far, turned)
    to_up, to_down, to_two = pack(
        (
            halves(0, 0, half) + [(2, chunk, 0, chunk), (3, chunk, 0, chunk), (4, 0, 0, block)],
            halves(1, half, half) + [(2, 3 * chunk, 0, chunk), (3, 3 * chunk, 0, chunk), (4, 0, 0, block)],
            [(2, 2 * chunk, 0, chunk), (3, 2 * chunk, 0, chunk), (4, 0, 0, block)],
        ),
        parts,
    )
    up2 = shift(to_up, "z", 1)
    down2 = shift(to_down, "z", -1)
    two2 = shift(to_two, "z", 2)
    wq_new, query = join(
        (
            (0, 0, 2 * half, "q", 0, 0, 0, 0, 2 * WIDTH),
            (1, 0, 2 * half, "q", 0, -1, 0, 0, 2 * WIDTH),
            (2, 0, 2 * half, "q", 0, 1, 0, 0, 2 * WIDTH),
        ),
        (wq_old, up, down),
        normed,
    )
    (to_across,) = pack(
        (halves(0, 0, F) + halves(1, 0, F) + [(2, 0, 0, block)],), (up, down, turned), (query,)
    )
    across2 = shift(to_across, "yl", 1)

    later = across[F:]
    up3 = shift(later, "z", 1)
    down3 = shift(later, "z", -1)
    page_rows = 2 * half
    wkv_at = page_rows + 2 * chunk
    (to_across3,) = pack(
        (
            [
                (0, 0, 0, F),
                (0, half, 0, F),
                (0, wkv_at, 0, block),
                (1, wkv_at, 0, block),
                (2, 2 * chunk, 0, block),
            ],
        ),
        (up2, down2, two2),
    )
    across3 = shift(to_across3, "yl", 1)
    wq_new, query = join(
        (
            (0, 0, 2 * half, "q", 1, 0, 0, 0, 2 * WIDTH),
            (1, 0, half, "q", 0, 2, 0, 0, WIDTH),
            (1, half, half, "q", 0, 2, 0, WIDTH, WIDTH),
            (2, 0, half, "q", 0, 2, half, 0, WIDTH),
            (2, half, half, "q", 0, 2, half, WIDTH, WIDTH),
            (3, 0, F, "q", 1, -1, 0, 0, WIDTH),
            (3, F, F, "q", 1, -1, 0, WIDTH, WIDTH),
            (3, 2 * F, F, "q", 1, 1, 0, 0, WIDTH),
            (3, 3 * F, F, "q", 1, 1, 0, WIDTH, WIDTH),
        ),
        (across, up2, down2, across2),
        normed,
        (wq_new, query),
    )
    stay, to_right, to_far, to_left = sort(
        (near, far, up2, down2, two2),
        [
            (0, 0, 0, 0),
            (1, 0, 0, chunk),
            (2, page_rows, 1, 0),
            (2, page_rows + chunk, 1, chunk),
            (3, page_rows, 3, 0),
            (3, page_rows + chunk, 3, chunk),
            (4, 0, 2, 0),
            (4, chunk, 2, chunk),
        ],
        chunk,
        (query,),
    )
    right = shift(to_right, "x", 1)
    left = shift(to_left, "x", -1)

    up4 = shift(up3[:split], "z", 1)
    down4 = shift(down3[split:], "z", -1)
    beyond = shift(to_far, "x", 2)
    wq_new, wkv_new, query, fresh = join(
        (
            (0, 0, rest, "q", 1, -1, F, 0, 2 * WIDTH),
            (1, 0, rest, "q", 1, 1, F, 0, 2 * WIDTH),
            (2, 0, F, "q", 1, 2, 0, 0, WIDTH),
            (2, F, F, "q", 1, 2, 0, WIDTH, WIDTH),
            (2, 2 * F, block, "own", 1, -1, 0, 0, WIDTH),
            (2, 2 * F + block, block, "own", 1, 1, 0, 0, WIDTH),
            (2, 2 * F + 2 * block, block, "own", 1, 2, 0, 0, WIDTH),
            (3, 0, block, "own", 0, 0, 0, 0, WIDTH),
            (4, wkv_at, block, "own", 0, -1, 0, 0, WIDTH),
            (5, wkv_at, block, "own", 0, 1, 0, 0, WIDTH),
            (6, 2 * chunk, block, "own", 0, 2, 0, 0, WIDTH),
            (7, 4 * F, block, "own", 1, 0, 0, 0, WIDTH),
        ),
        (up3, down3, across3, turned, up2, down2, two2, across2),
        normed,
        (wq_new, query),
    )
    to_core = staged(
            [
                (0, 0, 0, 2 * chunk),
                (1, 0, 0, 2 * chunk),
                (2, 0, 0, 2 * chunk),
                (3, 0, 0, block),
                (4, wkv_at, 0, block),
                (5, wkv_at, 0, block),
                (6, 2 * chunk, 0, block),
                (7, 4 * F, 0, block),
                (8, 2 * F, 0, 3 * block),
            ],
        (stay, right, left, turned, up2, down2, two2, across2, across3),
        (query,),
    )
    swapped = shift(to_core, "core", 1)
    swapped2 = shift(beyond, "core", 1)

    quarter = 2 * chunk
    base = 3 * quarter
    spots = ((0, 0), (0, -1), (0, 1), (0, 2), (1, 0), (1, -1), (1, 1), (1, 2))
    wq_new, wkv_new, kv_new, context = last(
        (
            *[
                (2, base + n * block, block, "other", dy, dz, 0, 0, WIDTH)
                for n, (dy, dz) in enumerate(spots)
            ],
            (0, 0, split, "q", 1, 2, F, 0, 2 * WIDTH),
            (1, 0, split, "q", 1, 2, F + split, 0, 2 * WIDTH),
        ),
        (up4, down4, swapped),
        [
            (0, 0, quarter, 0),
            (1, 0, quarter, quarter),
            (2, 0, quarter, 2 * quarter),
            (3, 0, quarter, 3 * quarter),
            (4, 0, quarter, 4 * quarter),
            (4, quarter, quarter, 5 * quarter),
            (5, 0, quarter, 6 * quarter),
            (4, 2 * quarter, quarter, 7 * quarter),
        ],
        (stay, right, beyond, left, swapped, swapped2),
        page,
        src,
        lengths,
        normed,
        cosine,
        sine,
        query,
        fresh,
        wq_new,
        wkv_new,
    )
    return (context, kv_new, wq_new, wkv_new)


def solution(mesh):
    torus = Mesh(mesh.devices.reshape(2, 4, 2, 4, 2), ("yl", "z", "yh", "x", "core"))
    return jax.shard_map(
        shards,
        mesh=torus,
        in_specs=(
            P(SECTION, None),
            P(),
            P(SECTION, TENSOR),
            P(TENSOR, SECTION),
            P(SECTION, TENSOR, None, None),
            P(),
            P(),
        ),
        out_specs=(
            P(SECTION, TENSOR),
            P(SECTION, TENSOR, None, None),
            P(None, TENSOR),
            P(None, TENSOR),
        ),
        check_vma=False,
    )
```

```python
import functools

import jax
import jax.numpy as jnp
from jax import lax
from jax.experimental import pallas as pl
from jax.experimental.pallas import tpu as pltpu
from jax.sharding import Mesh
from jax.sharding import PartitionSpec as P

KV_HEADS = 8
HEAD_DIM = 128
WIDTH = 2 * HEAD_DIM
SECTION = ("yl", "z")
TENSOR = ("yh", "x", "core")
EPSILON = 1e-05
ROPE_BASE = 500000.0
VMEM_LIMIT = 48 * 1024 * 1024

F = 256

ANY = pl.BlockSpec(memory_space=pl.ANY)
HBM = pl.BlockSpec(memory_space=pltpu.HBM)
VM = pl.BlockSpec(memory_space=pltpu.VMEM)
SM = pl.BlockSpec(memory_space=pltpu.SMEM)


def params():
    return pltpu.CompilerParams(vmem_limit_bytes=VMEM_LIMIT)


def cost(flops, nbytes):
    return pl.CostEstimate(flops=flops, bytes_accessed=nbytes, transcendentals=0)


def block_of(dy, dz):
    return lax.rem(lax.axis_index("yl") + dy, 2) * 4 + lax.rem(lax.axis_index("z") + dz + 4, 4)


def source_of(dy, dz):
    gap = lax.axis_index("z") + dz - lax.axis_index("x") + 8
    return lax.rem(lax.axis_index("yl") + dy, 2) * 4 + lax.rem(gap, 4)


def shift(value, axis, by):
    n = lax.axis_size(axis)
    return lax.ppermute(value, axis, [(i, (i + by) % n) for i in range(n)])


def pick_kernel(table_ref, kv_ref, _, *refs):
    out_refs, src_ref = refs[:2], refs[2]
    pool, picked, spots, spots_s, sems = refs[3:]
    reqs, width = table_ref.shape
    pages = kv_ref.shape[1]
    per_block = pages // reqs
    load = pltpu.make_async_copy(kv_ref.at[0], pool, sems.at[0])
    load.start()
    yl, z = lax.axis_index("yl"), lax.axis_index("z")
    yh, x, core = lax.axis_index("yh"), lax.axis_index("x"), lax.axis_index("core")
    table = table_ref[...]
    owner = table // pages
    local = table % pages
    before = lax.broadcasted_iota(jnp.int32, (width, width), 0)
    after = lax.broadcasted_iota(jnp.int32, (width, width), 1)
    tri = (before < after).astype(jnp.float32)
    mine = owner == yh * 8 + x * 2 + core
    rank = jnp.dot(mine.astype(jnp.float32), tri, preferred_element_type=jnp.float32)
    lanes = lax.broadcasted_iota(jnp.int32, (reqs, 128), 1)
    chosen = jnp.zeros((reqs, 128), jnp.int32)
    for k in range(per_block):
        hit = jnp.where(mine & (rank == k), local, 0)
        chosen = jnp.where(lanes == k, jnp.sum(hit, axis=1, keepdims=True), chosen)
    spots[...] = chosen
    move = pltpu.make_async_copy(spots, spots_s, sems.at[1])
    move.start()
    rows = src_ref.shape[0]
    first = pl.multiple_of((yl * 4 + z) * rows, rows)
    own = table_ref[pl.ds(first, rows), :] // pages
    ranks = jnp.zeros((rows, width), jnp.float32)
    for t in range(16):
        at = (own == t).astype(jnp.float32)
        ranks += at * jnp.dot(at, tri, preferred_element_type=jnp.float32)
    request = lax.broadcasted_iota(jnp.int32, (rows, width), 0)
    place = (own + core) % 2 * 4 + own // 2 % 4
    place = place * 2 + (own // 8 + yl) % 2
    place = (place * rows + request) * per_block
    src_ref[...] = place + ranks.astype(jnp.int32)
    move.wait()
    load.wait()
    outs = []
    for n in range(8):
        turn, dz = n // 4, n % 4
        start = (lax.rem(yh + turn, 2) * 4 + lax.rem(z + dz, 4)) * rows

        def body(i, _, n=n, start=start):
            for k in range(per_block):
                picked[(n * rows + i) * per_block + k] = pool[spots_s[start + i, k]]
            return 0

        lax.fori_loop(0, rows, body, 0)
        size = rows * per_block
        out = pltpu.make_async_copy(
            picked.at[pl.ds(n * size, size)],
            out_refs[turn].at[pl.ds(dz * size, size)],
            sems.at[2 + n],
        )
        out.start()
        outs.append(out)
    for out in outs:
        out.wait()


def pick(page_table, kv_old, after):
    pages, page, width = kv_old.shape[1:]
    reqs = page_table.shape[0]
    part = jax.ShapeDtypeStruct((pages // 2, page, width), jnp.bfloat16)
    return pl.pallas_call(
        pick_kernel,
        out_shape=(part, part, jax.ShapeDtypeStruct((reqs // 8, page_table.shape[1]), jnp.int32)),
        in_specs=[VM, HBM, ANY],
        out_specs=(ANY, ANY, VM),
        scratch_shapes=[
            pltpu.VMEM((pages, page, width), jnp.bfloat16),
            pltpu.VMEM((pages, page, width), jnp.bfloat16),
            pltpu.VMEM((reqs, 128), jnp.int32),
            pltpu.SMEM((reqs, 128), jnp.int32),
            pltpu.SemaphoreType.DMA((10,)),
        ],
        compiler_params=params(),
        cost_estimate=cost(0, 4 << 20),
    )(page_table, kv_old, after)


def staged_kernel(copies, sources, size, *refs):
    parts, out, stage, sems = refs[:sources], refs[-3], refs[-2], refs[-1]
    moves = []
    for n, (i, low, col, rows, _, at) in enumerate(copies):
        move = pltpu.make_async_copy(
            parts[i].at[pl.ds(low, rows), pl.ds(col, WIDTH)], stage.at[pl.ds(at, rows)], sems.at[n, 0]
        )
        move.start()
        moves.append(move)
    outs = []
    for n, (i, low, col, rows, _, at) in enumerate(copies):
        moves[n].wait()
        span = pl.ds(at, rows)
        move = pltpu.make_async_copy(stage.at[span], out.at[span], sems.at[n, 1])
        move.start()
        outs.append(move)
    for move in outs:
        move.wait()


def staged(layout, parts, after=()):
    copies, at = [], 0
    for i, low, col, rows in layout:
        copies.append((i, low, col, rows, 0, at))
        at += rows
    return pl.pallas_call(
        functools.partial(staged_kernel, tuple(copies), len(parts), at),
        out_shape=jax.ShapeDtypeStruct((at, WIDTH), jnp.bfloat16),
        in_specs=[ANY] * (len(parts) + len(after)),
        out_specs=ANY,
        scratch_shapes=[
            pltpu.VMEM((at, WIDTH), jnp.bfloat16),
            pltpu.SemaphoreType.DMA((len(copies), 2)),
        ],
        compiler_params=params(),
        cost_estimate=cost(0, at * WIDTH * 4),
    )(*parts, *after)


def pack_kernel(copies, sources, sizes, *refs):
    parts, outs, sems = refs[:sources], refs[-1 - len(sizes) : -1], refs[-1]
    moves = []
    for n, (i, low, col, rows, o, at) in enumerate(copies):
        move = pltpu.make_async_copy(
            parts[i].at[pl.ds(low, rows), pl.ds(col, WIDTH)],
            outs[o].at[pl.ds(at, rows)],
            sems.at[n],
        )
        move.start()
        moves.append(move)
    for move in moves:
        move.wait()


def pack(layouts, parts, after=()):
    copies, sizes = [], []
    for o, layout in enumerate(layouts):
        at = 0
        for i, low, col, rows in layout:
            copies.append((i, low, col, rows, o, at))
            at += rows
        sizes.append(at)
    return pl.pallas_call(
        functools.partial(pack_kernel, tuple(copies), len(parts), tuple(sizes)),
        out_shape=[jax.ShapeDtypeStruct((size, WIDTH), jnp.bfloat16) for size in sizes],
        in_specs=[ANY] * (len(parts) + len(after)),
        out_specs=[ANY] * len(sizes),
        scratch_shapes=[pltpu.SemaphoreType.DMA((len(copies),))],
        compiler_params=params(),
        cost_estimate=cost(0, sum(sizes) * WIDTH * 4),
    )(*parts, *after)


def sort_kernel(parts, lows, count, *refs):
    ins, out = refs[:parts], refs[-3]
    held, sems = refs[-2:]
    moves = []
    for n, (i, low, dz, at) in enumerate(lows):
        move = pltpu.make_async_copy(
            ins[i].at[pl.ds(low, count)], held.at[dz, pl.ds(at, count)], sems.at[n]
        )
        move.start()
        moves.append(move)
    for move in moves:
        move.wait()
    z = lax.axis_index("z") + 4
    moves = []
    for to in range(4):
        move = pltpu.make_async_copy(held.at[lax.rem(z - to, 4)], out.at[to], sems.at[to])
        move.start()
        moves.append(move)
    for move in moves:
        move.wait()


def sort(parts, lows, count, after=()):
    return pl.pallas_call(
        functools.partial(sort_kernel, len(parts), tuple(lows), count),
        out_shape=jax.ShapeDtypeStruct((4, 2 * count, WIDTH), jnp.bfloat16),
        in_specs=[ANY] * (len(parts) + len(after)),
        out_specs=ANY,
        scratch_shapes=[
            pltpu.VMEM((4, 2 * count, WIDTH), jnp.bfloat16),
            pltpu.SemaphoreType.DMA((len(lows),)),
        ],
        compiler_params=params(),
        cost_estimate=cost(0, 8 << 20),
    )(*parts, *after)


def land(plan, buffers, loads, wholes, normed_ref, query, fresh, sems):
    outs, waited = [], set()
    query = list(query)
    for n, (i, low, rows, kind, dy, dz, at, col, width) in enumerate(plan):
        if i not in waited:
            loads[i].wait()
            waited.add(i)
        if kind == "q":
            start = pl.multiple_of(block_of(dy, dz) * 1024 + at, 128)
            whole = wholes[0].at[pl.ds(start, rows), pl.ds(col, width)]
        else:
            core = lax.axis_index("core")
            half = core if kind == "own" else 1 - core
            start = pl.multiple_of((source_of(dy, dz) * 2 + half) * 512, 512)
            whole = wholes[1].at[pl.ds(start, rows)]
        out = pltpu.make_async_copy(buffers[i].at[pl.ds(low, rows)], whole, sems.at[n])
        out.start()
        outs.append(out)
        normed = normed_ref[:, pl.ds(start, rows)]
        for c in range(0, width, WIDTH):
            term = jnp.dot(
                normed,
                buffers[i][low : low + rows, c : c + WIDTH],
                preferred_element_type=jnp.float32,
            )
            if kind == "q":
                query[(col + c) // WIDTH] += term
            else:
                fresh += term
    return query, fresh, outs


def join_kernel(plan, count, state, *refs):
    parts, normed_ref = refs[:count], refs[count]
    rest = refs[count + 1 :]
    wholes_n = 2 if any(item[3] != "q" for item in plan) else 1
    rows, columns = normed_ref.shape[0], 2 * WIDTH
    if state:
        query_in, rest = rest[0], rest[2:]
        query = [query_in[:, :WIDTH], query_in[:, WIDTH:]]
    else:
        query = [jnp.zeros((rows, WIDTH), jnp.float32)] * 2
    wholes, rest = rest[:wholes_n], rest[wholes_n:]
    query_ref, rest = rest[0], rest[1:]
    if wholes_n == 2:
        fresh_ref, rest = rest[0], rest[1:]
    buffers, sem_in, sem_out = rest[:count], rest[count], rest[count + 1]
    loads = []
    for i in range(count):
        load = pltpu.make_async_copy(parts[i], buffers[i], sem_in.at[i])
        load.start()
        loads.append(load)
    fresh = jnp.zeros((rows, WIDTH), jnp.float32)
    query, fresh, outs = land(plan, buffers, loads, wholes, normed_ref, query, fresh, sem_out)
    query_ref[:, :WIDTH] = query[0]
    query_ref[:, WIDTH:] = query[1]
    if wholes_n == 2:
        fresh_ref[...] = fresh
    for out in outs:
        out.wait()


def join(plan, parts, normed, state=None):
    rows, depth = normed.shape
    kv = any(item[3] != "q" for item in plan)
    args = [*parts, normed]
    in_specs = [ANY] * len(parts) + [VM]
    aliases = {}
    if state is not None:
        whole, query = state
        args += [query, whole]
        in_specs += [VM, HBM]
        aliases = {len(parts) + 2: 0}
    out_shape = [jax.ShapeDtypeStruct((depth, 2 * WIDTH), jnp.bfloat16)]
    out_specs = [HBM]
    if kv:
        out_shape.append(jax.ShapeDtypeStruct((depth, WIDTH), jnp.bfloat16))
        out_specs.append(HBM)
    out_shape.append(jax.ShapeDtypeStruct((rows, 2 * WIDTH), jnp.float32))
    out_specs.append(VM)
    if kv:
        out_shape.append(jax.ShapeDtypeStruct((rows, WIDTH), jnp.float32))
        out_specs.append(VM)
    nbytes = sum(part.size * 4 for part in parts)
    return pl.pallas_call(
        functools.partial(join_kernel, plan, len(parts), state is not None),
        out_shape=out_shape,
        in_specs=in_specs,
        out_specs=out_specs,
        input_output_aliases=aliases,
        scratch_shapes=[pltpu.VMEM(part.shape, jnp.bfloat16) for part in parts]
        + [pltpu.SemaphoreType.DMA((len(parts),)), pltpu.SemaphoreType.DMA((len(plan),))],
        compiler_params=params(),
        cost_estimate=cost(0, nbytes),
    )(*args)


def turn(value, cosine, sine):
    return value * cosine + pltpu.roll(value, HEAD_DIM // 2, 1) * sine


def last_kernel(plan, count, pages, page, *refs):
    parts, pools = refs[:count], refs[count : count + len(pages)]
    rest = refs[count + len(pages) :]
    src_ref, lengths_ref, normed_ref, cos_ref, sin_ref, query_ref, fresh_ref = rest[:7]
    rest = rest[9:]
    wq_ref, wkv_ref, cache_ref, context_ref = rest[:4]
    rest = rest[4:]
    buffers, rest = rest[:count], rest[count:]
    held, built, heads, mixed, sem_in, sem_pool, sem_out, sem_cache = rest
    rows, slots = built.shape[:2]
    fills = []
    for n, (i, low, size, at) in enumerate(pages):
        fill = pltpu.make_async_copy(
            pools[n].at[pl.ds(low, size)], held.at[pl.ds(at, size)], sem_pool.at[n]
        )
        fill.start()
        fills.append(fill)
    loads = []
    for i in range(count):
        load = pltpu.make_async_copy(parts[i], buffers[i], sem_in.at[i])
        load.start()
        loads.append(load)
    query = [query_ref[:, :WIDTH], query_ref[:, WIDTH:]]
    query, fresh, outs = land(
        plan, buffers, loads, (wq_ref, wkv_ref), normed_ref, query, fresh_ref[...], sem_out
    )
    cosine, sine = cos_ref[...], sin_ref[...]
    fresh = jnp.concatenate(
        [turn(fresh[:, :HEAD_DIM], cosine, sine), fresh[:, HEAD_DIM:]], axis=1
    )
    count_q = 2 * WIDTH // HEAD_DIM
    heads[...] = jnp.zeros_like(heads)
    for h in range(count_q):
        value = query[h * HEAD_DIM // WIDTH]
        low = h * HEAD_DIM % WIDTH
        heads[:, h, :] = turn(value[:, low : low + HEAD_DIM], cosine, sine)
    for fill in fills:
        fill.wait()
    first = (lax.axis_index("yl") * 4 + lax.axis_index("z")) * rows
    for r in range(rows):

        def body(j, _, r=r):
            for n in range(8):
                at = pl.multiple_of((j * 8 + n) * page, page)
                low = pl.multiple_of(src_ref[r, j * 8 + n] * page, page)
                built[r, pl.ds(at, page), :] = held[pl.ds(low, page), :]
            return 0

        lax.fori_loop(0, slots // page // 8, body, 0)
        length = lengths_ref[first + r]
        at = pl.multiple_of(length // page * page, page)
        old = built[r, pl.ds(at, page), :]
        line = lax.broadcasted_iota(jnp.int32, old.shape, 0)
        new = jnp.broadcast_to(fresh[r : r + 1, :], old.shape)
        built[r, pl.ds(at, page), :] = jnp.where(
            line == length % page, new, old.astype(jnp.float32)
        ).astype(jnp.bfloat16)
        out = pltpu.make_async_copy(built.at[r], cache_ref.at[r, 0], sem_cache.at[r])
        out.start()
        outs.append(out)
    for r in range(rows):
        length = lengths_ref[first + r]
        scores = lax.dot_general(
            heads[r].astype(jnp.bfloat16),
            built[r, :, :HEAD_DIM],
            (((1,), (1,)), ((), ())),
            preferred_element_type=jnp.float32,
        ) * HEAD_DIM ** (-0.5)
        seen = lax.broadcasted_iota(jnp.int32, scores.shape, 1) <= length
        peak = jnp.max(jnp.where(seen, scores, -jnp.inf), axis=1, keepdims=True)
        weights = jnp.where(seen, jnp.exp(scores - peak), 0.0)
        probs = (weights / jnp.sum(weights, axis=1, keepdims=True)).astype(jnp.bfloat16)
        result = jnp.dot(probs, built[r, :, HEAD_DIM:], preferred_element_type=jnp.float32)
        for h in range(count_q):
            mixed[r : r + 1, h * HEAD_DIM : (h + 1) * HEAD_DIM] = result[h : h + 1, :]
    context_ref[...] = mixed[...].astype(jnp.bfloat16)
    for out in outs:
        out.wait()


def last(plan, parts, pages, pools, page, src, lengths, normed, cosine, sine, query, fresh, wq_new, wkv_new):
    rows = normed.shape[0]
    slots = src.shape[1] * page
    pools = [pools[item[0]] for item in pages]
    args = [*parts, *pools, src, lengths, normed, cosine, sine, query, fresh, wq_new, wkv_new]
    lead = len(parts) + len(pools)
    return pl.pallas_call(
        functools.partial(last_kernel, plan, len(parts), tuple(pages), page),
        out_shape=[
            jax.ShapeDtypeStruct(wq_new.shape, jnp.bfloat16),
            jax.ShapeDtypeStruct(wkv_new.shape, jnp.bfloat16),
            jax.ShapeDtypeStruct((rows, 1, slots, WIDTH), jnp.bfloat16),
            jax.ShapeDtypeStruct(query.shape, jnp.bfloat16),
        ],
        in_specs=[ANY] * lead + [SM, SM, VM, VM, VM, VM, VM, HBM, HBM],
        out_specs=[HBM, HBM, HBM, VM],
        input_output_aliases={lead + 7: 0, lead + 8: 1},
        scratch_shapes=[pltpu.VMEM(part.shape, jnp.bfloat16) for part in parts]
        + [
            pltpu.VMEM((rows * slots, WIDTH), jnp.bfloat16),
            pltpu.VMEM((rows, slots, WIDTH), jnp.bfloat16),
            pltpu.VMEM((rows, 8, HEAD_DIM), jnp.float32),
            pltpu.VMEM(query.shape, jnp.float32),
            pltpu.SemaphoreType.DMA((len(parts),)),
            pltpu.SemaphoreType.DMA((len(pages),)),
            pltpu.SemaphoreType.DMA((len(plan),)),
            pltpu.SemaphoreType.DMA((rows,)),
        ],
        compiler_params=params(),
        cost_estimate=cost(64 << 20, 16 << 20),
    )(*args)


def halves(part, low, rows):
    return [(part, low, 0, rows), (part, low, WIDTH, rows)]


def shards(hidden_state, norm_gain, wq_old, wkv_old, kv_old, page_table, lengths):
    rows = hidden_state.shape[0]
    page = kv_old.shape[2]
    half = wq_old.shape[0] // 2
    rest = wq_old.shape[0] - F
    split = rest // 2

    pairs = []
    for yl in range(2):
        for z in range(4):
            for yh in range(2):
                for x in range(4):
                    here = ((yl * 4 + z) * 2 + yh) * 4 + x
                    pairs.append((here, ((yh * 4 + (z + x) % 4) * 2 + yl) * 4 + x))
    moved = lax.ppermute(wkv_old, ("yl", "z", "yh", "x"), pairs)
    up = shift(wq_old, "z", 1)
    down = shift(wq_old, "z", -1)
    picked = pick(page_table, kv_old, moved)
    src = picked[2]
    near, far = [
        lax.ppermute(
            picked[flip].reshape(-1, WIDTH),
            ("yl", "yh"),
            [(a * 2 + b, (b ^ flip) * 2 + a) for a in range(2) for b in range(2)],
        )
        for flip in range(2)
    ]
    turned = lax.ppermute(
        moved, ("z", "x"), [(z * 4 + x, z * 4 + (z - x) % 4) for z in range(4) for x in range(4)]
    )
    across = shift(wq_old, "yl", 1)

    my_lengths = lax.dynamic_slice_in_dim(lengths, lax.axis_index(SECTION) * rows, rows, 0)
    widened = hidden_state.astype(jnp.float32)
    scale = lax.rsqrt(jnp.mean(widened * widened, axis=1, keepdims=True) + EPSILON)
    normed = (widened * scale * norm_gain[None, :]).astype(jnp.bfloat16)
    spread = HEAD_DIM // 2
    frequency = ROPE_BASE ** (-(jnp.arange(spread, dtype=jnp.float32) * 2.0 / HEAD_DIM))
    angles = my_lengths.astype(jnp.float32)[:, None] * frequency[None, :]
    cosine, sine = jnp.cos(angles), jnp.sin(angles)
    cosine = jnp.concatenate([cosine, cosine], axis=1)
    sine = jnp.concatenate([-sine, sine], axis=1)

    chunk = near.shape[0] // 4
    block = turned.shape[0]
    parts = (up, down, near, far, turned)
    to_up, to_down, to_two, to_across = pack(
        (
            halves(0, 0, half) + [(2, chunk, 0, chunk), (3, chunk, 0, chunk), (4, 0, 0, block)],
            halves(1, half, half) + [(2, 3 * chunk, 0, chunk), (3, 3 * chunk, 0, chunk), (4, 0, 0, block)],
            [(2, 2 * chunk, 0, chunk), (3, 2 * chunk, 0, chunk), (4, 0, 0, block)],
            halves(0, 0, F) + halves(1, 0, F) + [(4, 0, 0, block)],
        ),
        parts,
    )
    up2 = shift(to_up, "z", 1)
    down2 = shift(to_down, "z", -1)
    two2 = shift(to_two, "z", 2)
    wq_new, query = join(
        (
            (0, 0, 2 * half, "q", 0, 0, 0, 0, 2 * WIDTH),
            (1, 0, 2 * half, "q", 0, -1, 0, 0, 2 * WIDTH),
            (2, 0, 2 * half, "q", 0, 1, 0, 0, 2 * WIDTH),
        ),
        (wq_old, up, down),
        normed,
    )
    across2 = shift(to_across, "yl", 1)

    later = across[F:]
    up3 = shift(later, "z", 1)
    down3 = shift(later, "z", -1)
    page_rows = 2 * half
    wkv_at = page_rows + 2 * chunk
    (to_across3,) = pack(
        (
            [
                (0, 0, 0, F),
                (0, half, 0, F),
                (0, wkv_at, 0, block),
                (1, wkv_at, 0, block),
                (2, 2 * chunk, 0, block),
            ],
        ),
        (up2, down2, two2),
    )
    across3 = shift(to_across3, "yl", 1)
    sorted_pages = sort(
        (near, far, up2, down2, two2),
        [
            (0, 0, 0, 0),
            (1, 0, 0, chunk),
            (2, page_rows, 1, 0),
            (2, page_rows + chunk, 1, chunk),
            (3, page_rows, 3, 0),
            (3, page_rows + chunk, 3, chunk),
            (4, 0, 2, 0),
            (4, chunk, 2, chunk),
        ],
        chunk,
        (across, across2),
    )
    mine = lax.all_to_all(sorted_pages, "x", split_axis=0, concat_axis=0, tiled=True)
    wq_new, query = join(
        (
            (0, 0, 2 * half, "q", 1, 0, 0, 0, 2 * WIDTH),
            (1, 0, half, "q", 0, 2, 0, 0, WIDTH),
            (1, half, half, "q", 0, 2, 0, WIDTH, WIDTH),
            (2, 0, half, "q", 0, 2, half, 0, WIDTH),
            (2, half, half, "q", 0, 2, half, WIDTH, WIDTH),
            (3, 0, F, "q", 1, -1, 0, 0, WIDTH),
            (3, F, F, "q", 1, -1, 0, WIDTH, WIDTH),
            (3, 2 * F, F, "q", 1, 1, 0, 0, WIDTH),
            (3, 3 * F, F, "q", 1, 1, 0, WIDTH, WIDTH),
        ),
        (across, up2, down2, across2),
        normed,
        (wq_new, query),
    )
    to_core = staged(
        [
            (0, 0, 0, block),
            (1, wkv_at, 0, block),
            (2, wkv_at, 0, block),
            (3, 2 * chunk, 0, block),
            (4, 4 * F, 0, block),
        ],
        (turned, up2, down2, two2, across2),
    )
    swapped = shift(to_core, "core", 1)

    mine = mine.reshape(-1, WIDTH)
    other = shift(mine, "core", 1)
    swapped2 = shift(across3, "core", 1)
    up4 = shift(up3[:split], "z", 1)
    down4 = shift(down3[split:], "z", -1)
    wq_new, wkv_new, query, fresh = join(
        (
            (0, 0, rest, "q", 1, -1, F, 0, 2 * WIDTH),
            (1, 0, rest, "q", 1, 1, F, 0, 2 * WIDTH),
            (2, 0, F, "q", 1, 2, 0, 0, WIDTH),
            (2, F, F, "q", 1, 2, 0, WIDTH, WIDTH),
            (2, 2 * F, block, "own", 1, -1, 0, 0, WIDTH),
            (2, 2 * F + block, block, "own", 1, 1, 0, 0, WIDTH),
            (2, 2 * F + 2 * block, block, "own", 1, 2, 0, 0, WIDTH),
            (3, 0, block, "own", 0, 0, 0, 0, WIDTH),
            (4, wkv_at, block, "own", 0, -1, 0, 0, WIDTH),
            (5, wkv_at, block, "own", 0, 1, 0, 0, WIDTH),
            (6, 2 * chunk, block, "own", 0, 2, 0, 0, WIDTH),
            (7, 4 * F, block, "own", 1, 0, 0, 0, WIDTH),
        ),
        (up3, down3, across3, turned, up2, down2, two2, across2),
        normed,
        (wq_new, query),
    )

    spots = ((0, 0), (0, -1), (0, 1), (0, 2), (1, 0))
    spots2 = ((1, -1), (1, 1), (1, 2))
    wq_new, wkv_new, kv_new, context = last(
        (
            *[
                (2, n * block, block, "other", dy, dz, 0, 0, WIDTH)
                for n, (dy, dz) in enumerate(spots)
            ],
            *[
                (3, 2 * F + n * block, block, "other", dy, dz, 0, 0, WIDTH)
                for n, (dy, dz) in enumerate(spots2)
            ],
            (0, 0, split, "q", 1, 2, F, 0, 2 * WIDTH),
            (1, 0, split, "q", 1, 2, F + split, 0, 2 * WIDTH),
        ),
        (up4, down4, swapped, swapped2),
        [(0, 0, mine.shape[0], 0), (1, 0, mine.shape[0], mine.shape[0])],
        (mine, other),
        page,
        src,
        lengths,
        normed,
        cosine,
        sine,
        query,
        fresh,
        wq_new,
        wkv_new,
    )
    return (context, kv_new, wq_new, wkv_new)


def solution(mesh):
    torus = Mesh(mesh.devices.reshape(2, 4, 2, 4, 2), ("yl", "z", "yh", "x", "core"))
    return jax.shard_map(
        shards,
        mesh=torus,
        in_specs=(
            P(SECTION, None),
            P(),
            P(SECTION, TENSOR),
            P(TENSOR, SECTION),
            P(SECTION, TENSOR, None, None),
            P(),
            P(),
        ),
        out_specs=(
            P(SECTION, TENSOR),
            P(SECTION, TENSOR, None, None),
            P(None, TENSOR),
            P(None, TENSOR),
        ),
        check_vma=False,
    )
```

```python
import functools

import jax
import jax.numpy as jnp
from jax import lax
from jax.experimental import pallas as pl
from jax.experimental.pallas import tpu as pltpu
from jax.sharding import Mesh
from jax.sharding import PartitionSpec as P

KV_HEADS = 8
HEAD_DIM = 128
WIDTH = 2 * HEAD_DIM
SECTION = ("yl", "z")
TENSOR = ("yh", "x", "core")
EPSILON = 1e-05
ROPE_BASE = 500000.0
VMEM_LIMIT = 10 * 1024 * 1024
LAST_LIMIT = 16 * 1024 * 1024
BUSY = 4 * 10**10

F = 256

ANY = pl.BlockSpec(memory_space=pl.ANY)
HBM = pl.BlockSpec(memory_space=pltpu.HBM)
VM = pl.BlockSpec(memory_space=pltpu.VMEM)
SM = pl.BlockSpec(memory_space=pltpu.SMEM)


def params(limit=VMEM_LIMIT):
    return pltpu.CompilerParams(vmem_limit_bytes=limit)


def cost(flops, nbytes):
    return pl.CostEstimate(flops=flops, bytes_accessed=nbytes, transcendentals=0)


def block_of(dy, dz):
    return lax.rem(lax.axis_index("yl") + dy, 2) * 4 + lax.rem(lax.axis_index("z") + dz + 4, 4)


def source_of(dy, dz):
    gap = lax.axis_index("z") + dz - lax.axis_index("x") + 8
    return lax.rem(lax.axis_index("yl") + dy, 2) * 4 + lax.rem(gap, 4)


def shift(value, axis, by):
    n = lax.axis_size(axis)
    return lax.ppermute(value, axis, [(i, (i + by) % n) for i in range(n)])


def pick_kernel(table_ref, kv_ref, *refs):
    out_refs, src_ref = refs[:2], refs[2]
    picked, spots, spots_s, sems = refs[3:]
    reqs, width = table_ref.shape
    pages = kv_ref.shape[1]
    per_block = pages // reqs
    yl, z = lax.axis_index("yl"), lax.axis_index("z")
    yh, x, core = lax.axis_index("yh"), lax.axis_index("x"), lax.axis_index("core")
    table = table_ref[...]
    owner = table // pages
    local = table % pages
    before = lax.broadcasted_iota(jnp.int32, (width, width), 0)
    after = lax.broadcasted_iota(jnp.int32, (width, width), 1)
    tri = (before < after).astype(jnp.float32)
    mine = owner == yh * 8 + x * 2 + core
    rank = jnp.dot(mine.astype(jnp.float32), tri, preferred_element_type=jnp.float32)
    lanes = lax.broadcasted_iota(jnp.int32, (reqs, 128), 1)
    chosen = jnp.zeros((reqs, 128), jnp.int32)
    for k in range(per_block):
        hit = jnp.where(mine & (rank == k), local, 0)
        chosen = jnp.where(lanes == k, jnp.sum(hit, axis=1, keepdims=True), chosen)
    spots[...] = chosen
    move = pltpu.make_async_copy(spots, spots_s, sems.at[1])
    move.start()
    rows = src_ref.shape[0]
    first = pl.multiple_of((yl * 4 + z) * rows, rows)
    own = table_ref[pl.ds(first, rows), :] // pages
    ranks = jnp.zeros((rows, width), jnp.float32)
    for t in range(16):
        at = (own == t).astype(jnp.float32)
        ranks += at * jnp.dot(at, tri, preferred_element_type=jnp.float32)
    request = lax.broadcasted_iota(jnp.int32, (rows, width), 0)
    place = (own + core) % 2 * 4 + own // 2 % 4
    place = place * 2 + (own // 8 + yl) % 2
    place = (place * rows + request) * per_block
    src_ref[...] = place + ranks.astype(jnp.int32)
    move.wait()
    outs = []
    for n in range(8):
        turn, dz = n // 4, n % 4
        start = (lax.rem(yh + turn, 2) * 4 + lax.rem(z + dz, 4)) * rows

        def body(i, _, n=n, start=start):
            for k in range(per_block):
                picked[(n * rows + i) * per_block + k] = kv_ref[0, spots_s[start + i, k]]
            return 0

        lax.fori_loop(0, rows, body, 0)
        size = rows * per_block
        out = pltpu.make_async_copy(
            picked.at[pl.ds(n * size, size)],
            out_refs[turn].at[pl.ds(dz * size, size)],
            sems.at[2 + n],
        )
        out.start()
        outs.append(out)
    for out in outs:
        out.wait()


def pick(page_table, kv_old):
    pages, page, width = kv_old.shape[1:]
    reqs = page_table.shape[0]
    part = jax.ShapeDtypeStruct((pages // 2, page, width), jnp.bfloat16)
    return pl.pallas_call(
        pick_kernel,
        out_shape=(part, part, jax.ShapeDtypeStruct((reqs // 8, page_table.shape[1]), jnp.int32)),
        in_specs=[VM, VM],
        out_specs=(ANY, ANY, VM),
        scratch_shapes=[
            pltpu.VMEM((pages, page, width), jnp.bfloat16),
            pltpu.VMEM((reqs, 128), jnp.int32),
            pltpu.SMEM((reqs, 128), jnp.int32),
            pltpu.SemaphoreType.DMA((10,)),
        ],
        compiler_params=params(),
        cost_estimate=cost(BUSY, 4 << 20),
    )(page_table, kv_old)


def pack_kernel(copies, sources, outputs, *refs):
    parts, rest = refs[:sources], refs[-2 * outputs - 2 :]
    outs, stages, sem_in, sem_out = rest[:outputs], rest[outputs:-2], rest[-2], rest[-1]
    moves = []
    for n, (i, low, col, rows, o, at) in enumerate(copies):
        move = pltpu.make_async_copy(
            parts[i].at[pl.ds(low, rows), pl.ds(col, outs[o].shape[1])],
            stages[o].at[pl.ds(at, rows)],
            sem_in.at[n],
        )
        move.start()
        moves.append(move)
    sent = []
    for n, (_, _, _, rows, o, at) in enumerate(copies):
        moves[n].wait()
        span = pl.ds(at, rows)
        move = pltpu.make_async_copy(stages[o].at[span], outs[o].at[span], sem_out.at[n])
        move.start()
        sent.append(move)
    for move in sent:
        move.wait()


def pack(layouts, parts, after=(), widths=None):
    widths = widths or (WIDTH,) * len(layouts)
    copies, shapes = [], []
    for o, layout in enumerate(layouts):
        at = 0
        for i, low, col, rows in layout:
            copies.append((i, low, col, rows, o, at))
            at += rows
        shapes.append((at, widths[o]))
    return pl.pallas_call(
        functools.partial(pack_kernel, tuple(copies), len(parts), len(shapes)),
        out_shape=[jax.ShapeDtypeStruct(shape, jnp.bfloat16) for shape in shapes],
        in_specs=[ANY] * (len(parts) + len(after)),
        out_specs=[ANY] * len(shapes),
        scratch_shapes=[pltpu.VMEM(shape, jnp.bfloat16) for shape in shapes]
        + [pltpu.SemaphoreType.DMA((len(copies),)), pltpu.SemaphoreType.DMA((len(copies),))],
        compiler_params=params(),
        cost_estimate=cost(0, sum(a * b * 4 for a, b in shapes)),
    )(*parts, *after)


def sort_kernel(parts, lows, count, copies, *refs):
    ins, out, extras = refs[:parts], refs[-8], refs[-7:-5]
    held, sems, sem_extra = refs[-5], refs[-2], refs[-1]
    stages = refs[-4:-2]
    firsts = []
    for n, (i, low, rows, o, at) in enumerate(copies):
        move = pltpu.make_async_copy(
            ins[i].at[pl.ds(low, rows)], stages[o].at[pl.ds(at, rows)], sem_extra.at[n, 0]
        )
        move.start()
        firsts.append(move)
    moves = []
    for n, (i, low, dz, at) in enumerate(lows):
        move = pltpu.make_async_copy(
            ins[i].at[pl.ds(low, count)], held.at[dz, pl.ds(at, count)], sems.at[n]
        )
        move.start()
        moves.append(move)
    sent = []
    for n, (i, low, rows, o, at) in enumerate(copies):
        firsts[n].wait()
        span = pl.ds(at, rows)
        move = pltpu.make_async_copy(stages[o].at[span], extras[o].at[span], sem_extra.at[n, 1])
        move.start()
        sent.append(move)
    for move in moves:
        move.wait()
    z = lax.axis_index("z") + 4
    moves = []
    for to in range(4):
        move = pltpu.make_async_copy(held.at[lax.rem(z - to, 4)], out.at[to], sems.at[to])
        move.start()
        moves.append(move)
    for move in moves + sent:
        move.wait()


def sort(parts, lows, count, layouts, after=()):
    copies, shapes = [], []
    for o, layout in enumerate(layouts):
        at = 0
        for i, low, rows in layout:
            copies.append((i, low, rows, o, at))
            at += rows
        shapes.append((at, WIDTH))
    return pl.pallas_call(
        functools.partial(sort_kernel, len(parts), tuple(lows), count, tuple(copies)),
        out_shape=[
            jax.ShapeDtypeStruct((4, 2 * count, WIDTH), jnp.bfloat16),
            *[jax.ShapeDtypeStruct(shape, jnp.bfloat16) for shape in shapes],
        ],
        in_specs=[ANY] * (len(parts) + len(after)),
        out_specs=[ANY] * 3,
        scratch_shapes=[
            pltpu.VMEM((4, 2 * count, WIDTH), jnp.bfloat16),
            *[pltpu.VMEM(shape, jnp.bfloat16) for shape in shapes],
            pltpu.SemaphoreType.DMA((len(lows),)),
            pltpu.SemaphoreType.DMA((len(copies), 2)),
        ],
        compiler_params=params(),
        cost_estimate=cost(0, 8 << 20),
    )(*parts, *after)


def land(plan, buffers, loads, wholes, normed_ref, query, fresh, sems):
    outs, waited = [], set()
    query = list(query)
    for n, (i, low, rows, kind, dy, dz, at, col, width) in enumerate(plan):
        if i not in waited:
            loads[i].wait()
            waited.add(i)
        if kind == "q":
            start = pl.multiple_of(block_of(dy, dz) * 1024 + at, 128)
            whole = wholes[0].at[pl.ds(start, rows), pl.ds(col, width)]
        else:
            core = lax.axis_index("core")
            half = core if kind == "own" else 1 - core
            start = pl.multiple_of((source_of(dy, dz) * 2 + half) * 512, 512)
            whole = wholes[1].at[pl.ds(start, rows)]
        out = pltpu.make_async_copy(buffers[i].at[pl.ds(low, rows)], whole, sems.at[n])
        out.start()
        outs.append(out)
        normed = normed_ref[:, pl.ds(start, rows)]
        for c in range(0, width, WIDTH):
            term = jnp.dot(
                normed,
                buffers[i][low : low + rows, c : c + WIDTH],
                preferred_element_type=jnp.float32,
            )
            if kind == "q":
                query[(col + c) // WIDTH] += term
            else:
                fresh += term
    return query, fresh, outs


def join_kernel(plan, count, state, *refs):
    parts, normed_ref = refs[:count], refs[count]
    rest = refs[count + 1 :]
    wholes_n = 2 if any(item[3] != "q" for item in plan) else 1
    rows, columns = normed_ref.shape[0], 2 * WIDTH
    if state:
        query_in, rest = rest[0], rest[2:]
        query = [query_in[:, :WIDTH], query_in[:, WIDTH:]]
    else:
        query = [jnp.zeros((rows, WIDTH), jnp.float32)] * 2
    wholes, rest = rest[:wholes_n], rest[wholes_n:]
    query_ref, rest = rest[0], rest[1:]
    if wholes_n == 2:
        fresh_ref, rest = rest[0], rest[1:]
    buffers, sem_in, sem_out = rest[:count], rest[count], rest[count + 1]
    loads = []
    for i in range(count):
        load = pltpu.make_async_copy(parts[i], buffers[i], sem_in.at[i])
        load.start()
        loads.append(load)
    fresh = jnp.zeros((rows, WIDTH), jnp.float32)
    query, fresh, outs = land(plan, buffers, loads, wholes, normed_ref, query, fresh, sem_out)
    query_ref[:, :WIDTH] = query[0]
    query_ref[:, WIDTH:] = query[1]
    if wholes_n == 2:
        fresh_ref[...] = fresh
    for out in outs:
        out.wait()


def join(plan, parts, normed, state=None, after=(), busy=BUSY):
    rows, depth = normed.shape
    kv = any(item[3] != "q" for item in plan)
    args = [*parts, normed]
    in_specs = [ANY] * len(parts) + [VM]
    aliases = {}
    if state is not None:
        whole, query = state
        args += [query, whole]
        in_specs += [VM, HBM]
        aliases = {len(parts) + 2: 0}
    out_shape = [jax.ShapeDtypeStruct((depth, 2 * WIDTH), jnp.bfloat16)]
    out_specs = [HBM]
    if kv:
        out_shape.append(jax.ShapeDtypeStruct((depth, WIDTH), jnp.bfloat16))
        out_specs.append(HBM)
    out_shape.append(jax.ShapeDtypeStruct((rows, 2 * WIDTH), jnp.float32))
    out_specs.append(VM)
    if kv:
        out_shape.append(jax.ShapeDtypeStruct((rows, WIDTH), jnp.float32))
        out_specs.append(VM)
    nbytes = sum(part.size * 4 for part in parts)
    return pl.pallas_call(
        functools.partial(join_kernel, plan, len(parts), state is not None),
        out_shape=out_shape,
        in_specs=in_specs,
        out_specs=out_specs,
        input_output_aliases=aliases,
        scratch_shapes=[pltpu.VMEM(part.shape, jnp.bfloat16) for part in parts]
        + [pltpu.SemaphoreType.DMA((len(parts),)), pltpu.SemaphoreType.DMA((len(plan),))],
        compiler_params=params(),
        cost_estimate=cost(busy, nbytes),
    )(*args)


def turn(value, cosine, sine):
    return value * cosine + pltpu.roll(value, HEAD_DIM // 2, 1) * sine


def last_kernel(plan, count, pages, page, *refs):
    parts, pools = refs[:count], refs[count : count + len(pages)]
    rest = refs[count + len(pages) :]
    src_ref, lengths_ref, normed_ref, cos_ref, sin_ref, query_ref, fresh_ref = rest[:7]
    rest = rest[9:]
    wq_ref, wkv_ref, cache_ref, context_ref = rest[:4]
    rest = rest[4:]
    buffers, rest = rest[:count], rest[count:]
    held, built, heads, mixed, sem_in, sem_pool, sem_out, sem_cache = rest
    rows, slots = built.shape[:2]
    fills = []
    for n, (i, low, size, at) in enumerate(pages):
        fill = pltpu.make_async_copy(
            pools[n].at[pl.ds(low, size)], held.at[pl.ds(at, size)], sem_pool.at[n]
        )
        fill.start()
        fills.append(fill)
    loads = []
    for i in range(count):
        load = pltpu.make_async_copy(parts[i], buffers[i], sem_in.at[i])
        load.start()
        loads.append(load)
    query = [query_ref[:, :WIDTH], query_ref[:, WIDTH:]]
    query, fresh, outs = land(
        plan, buffers, loads, (wq_ref, wkv_ref), normed_ref, query, fresh_ref[...], sem_out
    )
    cosine, sine = cos_ref[...], sin_ref[...]
    fresh = jnp.concatenate(
        [turn(fresh[:, :HEAD_DIM], cosine, sine), fresh[:, HEAD_DIM:]], axis=1
    )
    count_q = 2 * WIDTH // HEAD_DIM
    heads[...] = jnp.zeros_like(heads)
    for h in range(count_q):
        value = query[h * HEAD_DIM // WIDTH]
        low = h * HEAD_DIM % WIDTH
        heads[:, h, :] = turn(value[:, low : low + HEAD_DIM], cosine, sine)
    for fill in fills:
        fill.wait()
    first = (lax.axis_index("yl") * 4 + lax.axis_index("z")) * rows
    for r in range(rows):

        def body(j, _, r=r):
            for n in range(8):
                at = pl.multiple_of((j * 8 + n) * page, page)
                low = pl.multiple_of(src_ref[r, j * 8 + n] * page, page)
                built[r, pl.ds(at, page), :] = held[pl.ds(low, page), :]
            return 0

        lax.fori_loop(0, slots // page // 8, body, 0)
        length = lengths_ref[first + r]
        at = pl.multiple_of(length // page * page, page)
        old = built[r, pl.ds(at, page), :]
        line = lax.broadcasted_iota(jnp.int32, old.shape, 0)
        new = jnp.broadcast_to(fresh[r : r + 1, :], old.shape)
        built[r, pl.ds(at, page), :] = jnp.where(
            line == length % page, new, old.astype(jnp.float32)
        ).astype(jnp.bfloat16)
        out = pltpu.make_async_copy(built.at[r], cache_ref.at[r, 0], sem_cache.at[r])
        out.start()
        outs.append(out)
    for r in range(rows):
        length = lengths_ref[first + r]
        scores = lax.dot_general(
            heads[r].astype(jnp.bfloat16),
            built[r, :, :HEAD_DIM],
            (((1,), (1,)), ((), ())),
            preferred_element_type=jnp.float32,
        ) * HEAD_DIM ** (-0.5)
        seen = lax.broadcasted_iota(jnp.int32, scores.shape, 1) <= length
        peak = jnp.max(jnp.where(seen, scores, -jnp.inf), axis=1, keepdims=True)
        weights = jnp.where(seen, jnp.exp(scores - peak), 0.0)
        probs = (weights / jnp.sum(weights, axis=1, keepdims=True)).astype(jnp.bfloat16)
        result = jnp.dot(probs, built[r, :, HEAD_DIM:], preferred_element_type=jnp.float32)
        for h in range(count_q):
            mixed[r : r + 1, h * HEAD_DIM : (h + 1) * HEAD_DIM] = result[h : h + 1, :]
    context_ref[...] = mixed[...].astype(jnp.bfloat16)
    for out in outs:
        out.wait()


def last(plan, parts, pages, pools, page, src, lengths, normed, cosine, sine, query, fresh, wq_new, wkv_new):
    rows = normed.shape[0]
    slots = src.shape[1] * page
    pools = [pools[item[0]] for item in pages]
    args = [*parts, *pools, src, lengths, normed, cosine, sine, query, fresh, wq_new, wkv_new]
    lead = len(parts) + len(pools)
    return pl.pallas_call(
        functools.partial(last_kernel, plan, len(parts), tuple(pages), page),
        out_shape=[
            jax.ShapeDtypeStruct(wq_new.shape, jnp.bfloat16),
            jax.ShapeDtypeStruct(wkv_new.shape, jnp.bfloat16),
            jax.ShapeDtypeStruct((rows, 1, slots, WIDTH), jnp.bfloat16),
            jax.ShapeDtypeStruct(query.shape, jnp.bfloat16),
        ],
        in_specs=[ANY] * lead + [SM, SM, VM, VM, VM, VM, VM, HBM, HBM],
        out_specs=[HBM, HBM, HBM, VM],
        input_output_aliases={lead + 7: 0, lead + 8: 1},
        scratch_shapes=[pltpu.VMEM(part.shape, jnp.bfloat16) for part in parts]
        + [
            pltpu.VMEM((rows * slots, WIDTH), jnp.bfloat16),
            pltpu.VMEM((rows, slots, WIDTH), jnp.bfloat16),
            pltpu.VMEM((rows, 8, HEAD_DIM), jnp.float32),
            pltpu.VMEM(query.shape, jnp.float32),
            pltpu.SemaphoreType.DMA((len(parts),)),
            pltpu.SemaphoreType.DMA((len(pages),)),
            pltpu.SemaphoreType.DMA((len(plan),)),
            pltpu.SemaphoreType.DMA((rows,)),
        ],
        compiler_params=params(LAST_LIMIT),
        cost_estimate=cost(64 << 20, 16 << 20),
    )(*args)


def halves(part, low, rows):
    return [(part, low, 0, rows), (part, low, WIDTH, rows)]


def shards(hidden_state, norm_gain, wq_old, wkv_old, kv_old, page_table, lengths):
    rows = hidden_state.shape[0]
    page = kv_old.shape[2]
    half = wq_old.shape[0] // 2
    rest = wq_old.shape[0] - F
    split = rest // 2

    pairs = []
    for yl in range(2):
        for z in range(4):
            for yh in range(2):
                for x in range(4):
                    here = ((yl * 4 + z) * 2 + yh) * 4 + x
                    pairs.append((here, ((yh * 4 + (z + x) % 4) * 2 + yl) * 4 + x))
    moved = lax.ppermute(wkv_old, ("yl", "z", "yh", "x"), pairs)
    up = shift(wq_old, "z", 1)
    down = shift(wq_old, "z", -1)
    picked = pick(page_table, kv_old)
    src = picked[2]
    near, far = [
        lax.ppermute(
            picked[flip].reshape(-1, WIDTH),
            ("yl", "yh"),
            [(a * 2 + b, (b ^ flip) * 2 + a) for a in range(2) for b in range(2)],
        )
        for flip in range(2)
    ]
    turned = lax.ppermute(
        moved, ("z", "x"), [(z * 4 + x, z * 4 + (z - x) % 4) for z in range(4) for x in range(4)]
    )

    my_lengths = lax.dynamic_slice_in_dim(lengths, lax.axis_index(SECTION) * rows, rows, 0)
    widened = hidden_state.astype(jnp.float32)
    scale = lax.rsqrt(jnp.mean(widened * widened, axis=1, keepdims=True) + EPSILON)
    normed = (widened * scale * norm_gain[None, :]).astype(jnp.bfloat16)
    spread = HEAD_DIM // 2
    frequency = ROPE_BASE ** (-(jnp.arange(spread, dtype=jnp.float32) * 2.0 / HEAD_DIM))
    angles = my_lengths.astype(jnp.float32)[:, None] * frequency[None, :]
    cosine, sine = jnp.cos(angles), jnp.sin(angles)
    cosine = jnp.concatenate([cosine, cosine], axis=1)
    sine = jnp.concatenate([-sine, sine], axis=1)

    chunk = near.shape[0] // 4
    block = turned.shape[0]
    parts = (up, down, near, far, turned)
    to_up, to_down, to_two, to_across, own = pack(
        (
            halves(0, 0, half) + [(2, chunk, 0, chunk), (3, chunk, 0, chunk), (4, 0, 0, block)],
            halves(1, half, half) + [(2, 3 * chunk, 0, chunk), (3, 3 * chunk, 0, chunk), (4, 0, 0, block)],
            [(2, 2 * chunk, 0, chunk), (3, 2 * chunk, 0, chunk), (4, 0, 0, block)],
            halves(0, 0, F) + halves(1, 0, F) + [(4, 0, 0, block)],
            [(5, 0, 0, 2 * half)],
        ),
        (*parts, wq_old),
        (),
        (WIDTH, WIDTH, WIDTH, WIDTH, 2 * WIDTH),
    )
    across = shift(own, "yl", 1)
    up2 = shift(to_up, "z", 1)
    down2 = shift(to_down, "z", -1)
    two2 = shift(to_two, "z", 2)
    wq_new, query = join(
        (
            (0, 0, 2 * half, "q", 0, 0, 0, 0, 2 * WIDTH),
            (1, 0, 2 * half, "q", 0, -1, 0, 0, 2 * WIDTH),
            (2, 0, 2 * half, "q", 0, 1, 0, 0, 2 * WIDTH),
        ),
        (wq_old, up, down),
        normed,
    )
    across2 = shift(to_across, "yl", 1)

    later = across[F:]
    up3 = shift(later, "z", 1)
    down3 = shift(later, "z", -1)
    page_rows = 2 * half
    wkv_at = page_rows + 2 * chunk
    sorted_pages, to_across3, to_core = sort(
        (near, far, up2, down2, two2, turned, across2),
        [
            (0, 0, 0, 0),
            (1, 0, 0, chunk),
            (2, page_rows, 1, 0),
            (2, page_rows + chunk, 1, chunk),
            (3, page_rows, 3, 0),
            (3, page_rows + chunk, 3, chunk),
            (4, 0, 2, 0),
            (4, chunk, 2, chunk),
        ],
        chunk,
        [
            [(2, 0, F), (2, half, F), (2, wkv_at, block), (3, wkv_at, block), (4, 2 * chunk, block)],
            [
                (5, 0, block),
                (2, wkv_at, block),
                (3, wkv_at, block),
                (4, 2 * chunk, block),
                (6, 4 * F, block),
            ],
        ],
        (across,),
    )
    across3 = shift(to_across3, "yl", 1)
    mine = lax.all_to_all(sorted_pages, "x", split_axis=0, concat_axis=0, tiled=True)
    wq_new, query = join(
        (
            (0, 0, 2 * half, "q", 1, 0, 0, 0, 2 * WIDTH),
            (1, 0, half, "q", 0, 2, 0, 0, WIDTH),
            (1, half, half, "q", 0, 2, 0, WIDTH, WIDTH),
            (2, 0, half, "q", 0, 2, half, 0, WIDTH),
            (2, half, half, "q", 0, 2, half, WIDTH, WIDTH),
            (3, 0, F, "q", 1, -1, 0, 0, WIDTH),
            (3, F, F, "q", 1, -1, 0, WIDTH, WIDTH),
            (3, 2 * F, F, "q", 1, 1, 0, 0, WIDTH),
            (3, 3 * F, F, "q", 1, 1, 0, WIDTH, WIDTH),
        ),
        (across, up2, down2, across2),
        normed,
        (wq_new, query),
    )
    swapped = shift(to_core, "core", 1)

    mine = mine.reshape(-1, WIDTH)
    other = shift(mine, "core", 1)
    swapped2 = shift(across3, "core", 1)
    to_up4, to_down4 = pack(
        ([(0, 0, 0, split)], [(1, split, 0, split)]), (up3, down3), (), (2 * WIDTH, 2 * WIDTH)
    )
    up4 = shift(to_up4, "z", 1)
    down4 = shift(to_down4, "z", -1)
    wq_new, wkv_new, query, fresh = join(
        (
            (0, 0, rest, "q", 1, -1, F, 0, 2 * WIDTH),
            (1, 0, rest, "q", 1, 1, F, 0, 2 * WIDTH),
            (2, 0, F, "q", 1, 2, 0, 0, WIDTH),
            (2, F, F, "q", 1, 2, 0, WIDTH, WIDTH),
            (2, 2 * F, block, "own", 1, -1, 0, 0, WIDTH),
            (2, 2 * F + block, block, "own", 1, 1, 0, 0, WIDTH),
            (2, 2 * F + 2 * block, block, "own", 1, 2, 0, 0, WIDTH),
            (3, 0, block, "own", 0, 0, 0, 0, WIDTH),
            (3, block, block, "own", 0, -1, 0, 0, WIDTH),
            (3, 2 * block, block, "own", 0, 1, 0, 0, WIDTH),
            (3, 3 * block, block, "own", 0, 2, 0, 0, WIDTH),
            (3, 4 * block, block, "own", 1, 0, 0, 0, WIDTH),
        ),
        (up3, down3, across3, to_core),
        normed,
        (wq_new, query),
    )

    spots = ((0, 0), (0, -1), (0, 1), (0, 2), (1, 0))
    spots2 = ((1, -1), (1, 1), (1, 2))
    wq_new, wkv_new, kv_new, context = last(
        (
            *[
                (2, n * block, block, "other", dy, dz, 0, 0, WIDTH)
                for n, (dy, dz) in enumerate(spots)
            ],
            *[
                (3, 2 * F + n * block, block, "other", dy, dz, 0, 0, WIDTH)
                for n, (dy, dz) in enumerate(spots2)
            ],
            (0, 0, split, "q", 1, 2, F, 0, 2 * WIDTH),
            (1, 0, split, "q", 1, 2, F + split, 0, 2 * WIDTH),
        ),
        (up4, down4, swapped, swapped2),
        [(0, 0, mine.shape[0], 0), (1, 0, mine.shape[0], mine.shape[0])],
        (mine, other),
        page,
        src,
        lengths,
        normed,
        cosine,
        sine,
        query,
        fresh,
        wq_new,
        wkv_new,
    )
    return (context, kv_new, wq_new, wkv_new)


def solution(mesh):
    torus = Mesh(mesh.devices.reshape(2, 4, 2, 4, 2), ("yl", "z", "yh", "x", "core"))
    return jax.shard_map(
        shards,
        mesh=torus,
        in_specs=(
            P(SECTION, None),
            P(),
            P(SECTION, TENSOR),
            P(TENSOR, SECTION),
            P(SECTION, TENSOR, None, None),
            P(),
            P(),
        ),
        out_specs=(
            P(SECTION, TENSOR),
            P(SECTION, TENSOR, None, None),
            P(None, TENSOR),
            P(None, TENSOR),
        ),
        check_vma=False,
    )
```

```python
import functools

import jax
import jax.numpy as jnp
from jax import lax
from jax.experimental import pallas as pl
from jax.experimental.pallas import tpu as pltpu
from jax.sharding import Mesh
from jax.sharding import PartitionSpec as P

KV_HEADS = 8
HEAD_DIM = 128
WIDTH = 2 * HEAD_DIM
SECTION = ("yl", "z")
TENSOR = ("yh", "x", "core")
EPSILON = 1e-05
ROPE_BASE = 500000.0
VMEM_LIMIT = 10 * 1024 * 1024
LAST_LIMIT = 16 * 1024 * 1024
BUSY = 4 * 10**10

F = 256

ANY = pl.BlockSpec(memory_space=pl.ANY)
HBM = pl.BlockSpec(memory_space=pltpu.HBM)
VM = pl.BlockSpec(memory_space=pltpu.VMEM)
SM = pl.BlockSpec(memory_space=pltpu.SMEM)


def params(limit=VMEM_LIMIT):
    return pltpu.CompilerParams(vmem_limit_bytes=limit)


def cost(flops, nbytes):
    return pl.CostEstimate(flops=flops, bytes_accessed=nbytes, transcendentals=0)


def block_of(dy, dz):
    return lax.rem(lax.axis_index("yl") + dy, 2) * 4 + lax.rem(lax.axis_index("z") + dz + 4, 4)


def source_of(dy, dz):
    gap = lax.axis_index("z") + dz - lax.axis_index("x") + 8
    return lax.rem(lax.axis_index("yl") + dy, 2) * 4 + lax.rem(gap, 4)


def shift(value, axis, by):
    n = lax.axis_size(axis)
    return lax.ppermute(value, axis, [(i, (i + by) % n) for i in range(n)])


def pick_kernel(table_ref, kv_ref, *refs):
    out_refs, src_ref = refs[:2], refs[2]
    picked, spots, spots_s, sems = refs[3:]
    reqs, width = table_ref.shape
    pages = kv_ref.shape[1]
    per_block = pages // reqs
    yl, z = lax.axis_index("yl"), lax.axis_index("z")
    yh, x, core = lax.axis_index("yh"), lax.axis_index("x"), lax.axis_index("core")
    table = table_ref[...]
    owner = table // pages
    local = table % pages
    before = lax.broadcasted_iota(jnp.int32, (width, width), 0)
    after = lax.broadcasted_iota(jnp.int32, (width, width), 1)
    tri = (before < after).astype(jnp.float32)
    mine = owner == yh * 8 + x * 2 + core
    rank = jnp.dot(mine.astype(jnp.float32), tri, preferred_element_type=jnp.float32)
    lanes = lax.broadcasted_iota(jnp.int32, (reqs, 128), 1)
    chosen = jnp.zeros((reqs, 128), jnp.int32)
    for k in range(per_block):
        hit = jnp.where(mine & (rank == k), local, 0)
        chosen = jnp.where(lanes == k, jnp.sum(hit, axis=1, keepdims=True), chosen)
    spots[...] = chosen
    move = pltpu.make_async_copy(spots, spots_s, sems.at[1])
    move.start()
    rows = src_ref.shape[0]
    first = pl.multiple_of((yl * 4 + z) * rows, rows)
    own = table_ref[pl.ds(first, rows), :] // pages
    ranks = jnp.zeros((rows, width), jnp.float32)
    for t in range(16):
        at = (own == t).astype(jnp.float32)
        ranks += at * jnp.dot(at, tri, preferred_element_type=jnp.float32)
    request = lax.broadcasted_iota(jnp.int32, (rows, width), 0)
    place = (own + core) % 2 * 4 + own // 2 % 4
    place = place * 2 + (own // 8 + yl) % 2
    place = (place * rows + request) * per_block
    src_ref[...] = place + ranks.astype(jnp.int32)
    move.wait()
    outs = []
    for n in range(8):
        turn, dz = n // 4, n % 4
        start = (lax.rem(yh + turn, 2) * 4 + lax.rem(z + dz, 4)) * rows

        def body(i, _, n=n, start=start):
            for k in range(per_block):
                picked[(n * rows + i) * per_block + k] = kv_ref[0, spots_s[start + i, k]]
            return 0

        lax.fori_loop(0, rows, body, 0)
        size = rows * per_block
        out = pltpu.make_async_copy(
            picked.at[pl.ds(n * size, size)],
            out_refs[turn].at[pl.ds(dz * size, size)],
            sems.at[2 + n],
        )
        out.start()
        outs.append(out)
    for out in outs:
        out.wait()


def pick(page_table, kv_old):
    pages, page, width = kv_old.shape[1:]
    reqs = page_table.shape[0]
    part = jax.ShapeDtypeStruct((pages // 2, page, width), jnp.bfloat16)
    return pl.pallas_call(
        pick_kernel,
        out_shape=(part, part, jax.ShapeDtypeStruct((reqs // 8, page_table.shape[1]), jnp.int32)),
        in_specs=[VM, VM],
        out_specs=(ANY, ANY, VM),
        scratch_shapes=[
            pltpu.VMEM((pages, page, width), jnp.bfloat16),
            pltpu.VMEM((reqs, 128), jnp.int32),
            pltpu.SMEM((reqs, 128), jnp.int32),
            pltpu.SemaphoreType.DMA((10,)),
        ],
        compiler_params=params(),
        cost_estimate=cost(BUSY, 4 << 20),
    )(page_table, kv_old)


def pack_kernel(copies, sources, outputs, *refs):
    parts, rest = refs[:sources], refs[-2 * outputs - 2 :]
    outs, stages, sem_in, sem_out = rest[:outputs], rest[outputs:-2], rest[-2], rest[-1]
    moves = []
    for n, (i, low, col, rows, o, at) in enumerate(copies):
        move = pltpu.make_async_copy(
            parts[i].at[pl.ds(low, rows), pl.ds(col, outs[o].shape[1])],
            stages[o].at[pl.ds(at, rows)],
            sem_in.at[n],
        )
        move.start()
        moves.append(move)
    sent = []
    for n, (_, _, _, rows, o, at) in enumerate(copies):
        moves[n].wait()
        span = pl.ds(at, rows)
        move = pltpu.make_async_copy(stages[o].at[span], outs[o].at[span], sem_out.at[n])
        move.start()
        sent.append(move)
    for move in sent:
        move.wait()


def pack(layouts, parts, after=(), widths=None):
    widths = widths or (WIDTH,) * len(layouts)
    copies, shapes = [], []
    for o, layout in enumerate(layouts):
        at = 0
        for i, low, col, rows in layout:
            copies.append((i, low, col, rows, o, at))
            at += rows
        shapes.append((at, widths[o]))
    return pl.pallas_call(
        functools.partial(pack_kernel, tuple(copies), len(parts), len(shapes)),
        out_shape=[jax.ShapeDtypeStruct(shape, jnp.bfloat16) for shape in shapes],
        in_specs=[ANY] * (len(parts) + len(after)),
        out_specs=[ANY] * len(shapes),
        scratch_shapes=[pltpu.VMEM(shape, jnp.bfloat16) for shape in shapes]
        + [pltpu.SemaphoreType.DMA((len(copies),)), pltpu.SemaphoreType.DMA((len(copies),))],
        compiler_params=params(),
        cost_estimate=cost(0, sum(a * b * 4 for a, b in shapes)),
    )(*parts, *after)


def sort_kernel(parts, lows, count, copies, *refs):
    ins, out, extras = refs[:parts], refs[-8], refs[-7:-5]
    held, sems, sem_extra = refs[-5], refs[-2], refs[-1]
    stages = refs[-4:-2]
    firsts = []
    for n, (i, low, rows, o, at) in enumerate(copies):
        move = pltpu.make_async_copy(
            ins[i].at[pl.ds(low, rows)], stages[o].at[pl.ds(at, rows)], sem_extra.at[n, 0]
        )
        move.start()
        firsts.append(move)
    moves = []
    for n, (i, low, dz, at) in enumerate(lows):
        move = pltpu.make_async_copy(
            ins[i].at[pl.ds(low, count)], held.at[dz, pl.ds(at, count)], sems.at[n]
        )
        move.start()
        moves.append(move)
    sent = []
    for n, (i, low, rows, o, at) in enumerate(copies):
        firsts[n].wait()
        span = pl.ds(at, rows)
        move = pltpu.make_async_copy(stages[o].at[span], extras[o].at[span], sem_extra.at[n, 1])
        move.start()
        sent.append(move)
    for move in moves:
        move.wait()
    z = lax.axis_index("z") + 4
    moves = []
    for to in range(4):
        move = pltpu.make_async_copy(held.at[lax.rem(z - to, 4)], out.at[to], sems.at[to])
        move.start()
        moves.append(move)
    for move in moves + sent:
        move.wait()


def sort(parts, lows, count, layouts, after=()):
    copies, shapes = [], []
    for o, layout in enumerate(layouts):
        at = 0
        for i, low, rows in layout:
            copies.append((i, low, rows, o, at))
            at += rows
        shapes.append((at, WIDTH))
    return pl.pallas_call(
        functools.partial(sort_kernel, len(parts), tuple(lows), count, tuple(copies)),
        out_shape=[
            jax.ShapeDtypeStruct((4, 2 * count, WIDTH), jnp.bfloat16),
            *[jax.ShapeDtypeStruct(shape, jnp.bfloat16) for shape in shapes],
        ],
        in_specs=[ANY] * (len(parts) + len(after)),
        out_specs=[ANY] * 3,
        scratch_shapes=[
            pltpu.VMEM((4, 2 * count, WIDTH), jnp.bfloat16),
            *[pltpu.VMEM(shape, jnp.bfloat16) for shape in shapes],
            pltpu.SemaphoreType.DMA((len(lows),)),
            pltpu.SemaphoreType.DMA((len(copies), 2)),
        ],
        compiler_params=params(),
        cost_estimate=cost(0, 8 << 20),
    )(*parts, *after)


def land(plan, buffers, loads, wholes, normed_ref, query, fresh, sems):
    outs, waited = [], set()
    query = list(query)
    for n, (i, low, rows, kind, dy, dz, at, col, width) in enumerate(plan):
        if i not in waited:
            loads[i].wait()
            waited.add(i)
        if kind == "q":
            start = pl.multiple_of(block_of(dy, dz) * 1024 + at, 128)
            whole = wholes[0].at[pl.ds(start, rows), pl.ds(col, width)]
        else:
            core = lax.axis_index("core")
            half = core if kind == "own" else 1 - core
            start = pl.multiple_of((source_of(dy, dz) * 2 + half) * 512, 512)
            whole = wholes[1].at[pl.ds(start, rows)]
        out = pltpu.make_async_copy(buffers[i].at[pl.ds(low, rows)], whole, sems.at[n])
        out.start()
        outs.append(out)
        normed = normed_ref[:, pl.ds(start, rows)]
        for c in range(0, width, WIDTH):
            term = jnp.dot(
                normed,
                buffers[i][low : low + rows, c : c + WIDTH],
                preferred_element_type=jnp.float32,
            )
            if kind == "q":
                query[(col + c) // WIDTH] += term
            else:
                fresh += term
    return query, fresh, outs


def join_kernel(plan, count, state, *refs):
    parts, normed_ref = refs[:count], refs[count]
    rest = refs[count + 1 :]
    wholes_n = 2 if any(item[3] != "q" for item in plan) else 1
    rows, columns = normed_ref.shape[0], 2 * WIDTH
    if state:
        query_in, rest = rest[0], rest[2:]
        query = [query_in[:, :WIDTH], query_in[:, WIDTH:]]
    else:
        query = [jnp.zeros((rows, WIDTH), jnp.float32)] * 2
    wholes, rest = rest[:wholes_n], rest[wholes_n:]
    query_ref, rest = rest[0], rest[1:]
    if wholes_n == 2:
        fresh_ref, rest = rest[0], rest[1:]
    buffers, sem_in, sem_out = rest[:count], rest[count], rest[count + 1]
    loads = []
    for i in range(count):
        load = pltpu.make_async_copy(parts[i], buffers[i], sem_in.at[i])
        load.start()
        loads.append(load)
    fresh = jnp.zeros((rows, WIDTH), jnp.float32)
    query, fresh, outs = land(plan, buffers, loads, wholes, normed_ref, query, fresh, sem_out)
    query_ref[:, :WIDTH] = query[0]
    query_ref[:, WIDTH:] = query[1]
    if wholes_n == 2:
        fresh_ref[...] = fresh
    for out in outs:
        out.wait()


def join(plan, parts, normed, state=None, after=(), busy=BUSY):
    rows, depth = normed.shape
    kv = any(item[3] != "q" for item in plan)
    args = [*parts, normed]
    in_specs = [ANY] * len(parts) + [VM]
    aliases = {}
    if state is not None:
        whole, query = state
        args += [query, whole]
        in_specs += [VM, HBM]
        aliases = {len(parts) + 2: 0}
    out_shape = [jax.ShapeDtypeStruct((depth, 2 * WIDTH), jnp.bfloat16)]
    out_specs = [HBM]
    if kv:
        out_shape.append(jax.ShapeDtypeStruct((depth, WIDTH), jnp.bfloat16))
        out_specs.append(HBM)
    out_shape.append(jax.ShapeDtypeStruct((rows, 2 * WIDTH), jnp.float32))
    out_specs.append(VM)
    if kv:
        out_shape.append(jax.ShapeDtypeStruct((rows, WIDTH), jnp.float32))
        out_specs.append(VM)
    nbytes = sum(part.size * 4 for part in parts)
    return pl.pallas_call(
        functools.partial(join_kernel, plan, len(parts), state is not None),
        out_shape=out_shape,
        in_specs=in_specs,
        out_specs=out_specs,
        input_output_aliases=aliases,
        scratch_shapes=[pltpu.VMEM(part.shape, jnp.bfloat16) for part in parts]
        + [pltpu.SemaphoreType.DMA((len(parts),)), pltpu.SemaphoreType.DMA((len(plan),))],
        compiler_params=params(),
        cost_estimate=cost(busy, nbytes),
    )(*args)


def turn(value, cosine, sine):
    return value * cosine + pltpu.roll(value, HEAD_DIM // 2, 1) * sine


def last_kernel(plan, count, page, *refs):
    parts, (mine_ref, other_ref) = refs[:count], refs[count : count + 2]
    rest = refs[count + 2 :]
    src_ref, lengths_ref, normed_ref, cos_ref, sin_ref, query_ref, fresh_ref = rest[:7]
    rest = rest[9:]
    wq_ref, wkv_ref, cache_ref, context_ref = rest[:4]
    rest = rest[4:]
    buffers, rest = rest[:count], rest[count:]
    built, heads, mixed, sem_in, sem_out, sem_cache = rest
    rows, slots = built.shape[:2]
    loads = []
    for i in range(count):
        load = pltpu.make_async_copy(parts[i], buffers[i], sem_in.at[i])
        load.start()
        loads.append(load)
    total = mine_ref.shape[0] // page
    for r in range(rows):

        def body(j, _, r=r):
            for n in range(8):
                at = pl.multiple_of((j * 8 + n) * page, page)
                place = src_ref[r, j * 8 + n]
                low = pl.multiple_of(place % total * page, page)
                near = mine_ref[pl.ds(low, page), :]
                far = other_ref[pl.ds(low, page), :]
                built[r, pl.ds(at, page), :] = jnp.where(place < total, near, far)
            return 0

        lax.fori_loop(0, slots // page // 8, body, 0)
    query = [query_ref[:, :WIDTH], query_ref[:, WIDTH:]]
    query, fresh, outs = land(
        plan, buffers, loads, (wq_ref, wkv_ref), normed_ref, query, fresh_ref[...], sem_out
    )
    cosine, sine = cos_ref[...], sin_ref[...]
    fresh = jnp.concatenate(
        [turn(fresh[:, :HEAD_DIM], cosine, sine), fresh[:, HEAD_DIM:]], axis=1
    )
    count_q = 2 * WIDTH // HEAD_DIM
    heads[...] = jnp.zeros_like(heads)
    for h in range(count_q):
        value = query[h * HEAD_DIM // WIDTH]
        low = h * HEAD_DIM % WIDTH
        heads[:, h, :] = turn(value[:, low : low + HEAD_DIM], cosine, sine)
    first = (lax.axis_index("yl") * 4 + lax.axis_index("z")) * rows
    for r in range(rows):
        length = lengths_ref[first + r]
        at = pl.multiple_of(length // page * page, page)
        old = built[r, pl.ds(at, page), :]
        line = lax.broadcasted_iota(jnp.int32, old.shape, 0)
        new = jnp.broadcast_to(fresh[r : r + 1, :], old.shape)
        built[r, pl.ds(at, page), :] = jnp.where(
            line == length % page, new, old.astype(jnp.float32)
        ).astype(jnp.bfloat16)
        out = pltpu.make_async_copy(built.at[r], cache_ref.at[r, 0], sem_cache.at[r])
        out.start()
        outs.append(out)
    for r in range(rows):
        length = lengths_ref[first + r]
        scores = lax.dot_general(
            heads[r].astype(jnp.bfloat16),
            built[r, :, :HEAD_DIM],
            (((1,), (1,)), ((), ())),
            preferred_element_type=jnp.float32,
        ) * HEAD_DIM ** (-0.5)
        seen = lax.broadcasted_iota(jnp.int32, scores.shape, 1) <= length
        peak = jnp.max(jnp.where(seen, scores, -jnp.inf), axis=1, keepdims=True)
        weights = jnp.where(seen, jnp.exp(scores - peak), 0.0)
        probs = (weights / jnp.sum(weights, axis=1, keepdims=True)).astype(jnp.bfloat16)
        result = jnp.dot(probs, built[r, :, HEAD_DIM:], preferred_element_type=jnp.float32)
        for h in range(count_q):
            mixed[r : r + 1, h * HEAD_DIM : (h + 1) * HEAD_DIM] = result[h : h + 1, :]
    context_ref[...] = mixed[...].astype(jnp.bfloat16)
    for out in outs:
        out.wait()


def last(plan, parts, pools, page, src, lengths, normed, cosine, sine, query, fresh, wq_new, wkv_new):
    rows = normed.shape[0]
    slots = src.shape[1] * page
    args = [*parts, *pools, src, lengths, normed, cosine, sine, query, fresh, wq_new, wkv_new]
    lead = len(parts) + len(pools)
    return pl.pallas_call(
        functools.partial(last_kernel, plan, len(parts), page),
        out_shape=[
            jax.ShapeDtypeStruct(wq_new.shape, jnp.bfloat16),
            jax.ShapeDtypeStruct(wkv_new.shape, jnp.bfloat16),
            jax.ShapeDtypeStruct((rows, 1, slots, WIDTH), jnp.bfloat16),
            jax.ShapeDtypeStruct(query.shape, jnp.bfloat16),
        ],
        in_specs=[ANY] * len(parts) + [VM, VM, SM, SM, VM, VM, VM, VM, VM, HBM, HBM],
        out_specs=[HBM, HBM, HBM, VM],
        input_output_aliases={lead + 7: 0, lead + 8: 1},
        scratch_shapes=[pltpu.VMEM(part.shape, jnp.bfloat16) for part in parts]
        + [
            pltpu.VMEM((rows, slots, WIDTH), jnp.bfloat16),
            pltpu.VMEM((rows, 8, HEAD_DIM), jnp.float32),
            pltpu.VMEM(query.shape, jnp.float32),
            pltpu.SemaphoreType.DMA((len(parts),)),
            pltpu.SemaphoreType.DMA((len(plan),)),
            pltpu.SemaphoreType.DMA((rows,)),
        ],
        compiler_params=params(LAST_LIMIT),
        cost_estimate=cost(64 << 20, 16 << 20),
    )(*args)


def halves(part, low, rows):
    return [(part, low, 0, rows), (part, low, WIDTH, rows)]


def shards(hidden_state, norm_gain, wq_old, wkv_old, kv_old, page_table, lengths):
    rows = hidden_state.shape[0]
    page = kv_old.shape[2]
    half = wq_old.shape[0] // 2
    rest = wq_old.shape[0] - F
    split = rest // 2

    pairs = []
    for yl in range(2):
        for z in range(4):
            for yh in range(2):
                for x in range(4):
                    here = ((yl * 4 + z) * 2 + yh) * 4 + x
                    pairs.append((here, ((yh * 4 + (z + x) % 4) * 2 + yl) * 4 + x))
    moved = lax.ppermute(wkv_old, ("yl", "z", "yh", "x"), pairs)
    (held,) = pack(([(0, 0, 0, wq_old.shape[0])],), (wq_old,), (moved,), (2 * WIDTH,))
    up = shift(held, "z", 1)
    down = shift(held, "z", -1)
    picked = pick(page_table, kv_old)
    src = picked[2]
    near, far = [
        lax.ppermute(
            picked[flip].reshape(-1, WIDTH),
            ("yl", "yh"),
            [(a * 2 + b, (b ^ flip) * 2 + a) for a in range(2) for b in range(2)],
        )
        for flip in range(2)
    ]
    turned = lax.ppermute(
        moved, ("z", "x"), [(z * 4 + x, z * 4 + (z - x) % 4) for z in range(4) for x in range(4)]
    )

    my_lengths = lax.dynamic_slice_in_dim(lengths, lax.axis_index(SECTION) * rows, rows, 0)
    widened = hidden_state.astype(jnp.float32)
    scale = lax.rsqrt(jnp.mean(widened * widened, axis=1, keepdims=True) + EPSILON)
    normed = (widened * scale * norm_gain[None, :]).astype(jnp.bfloat16)
    spread = HEAD_DIM // 2
    frequency = ROPE_BASE ** (-(jnp.arange(spread, dtype=jnp.float32) * 2.0 / HEAD_DIM))
    angles = my_lengths.astype(jnp.float32)[:, None] * frequency[None, :]
    cosine, sine = jnp.cos(angles), jnp.sin(angles)
    cosine = jnp.concatenate([cosine, cosine], axis=1)
    sine = jnp.concatenate([-sine, sine], axis=1)

    chunk = near.shape[0] // 4
    block = turned.shape[0]
    parts = (up, down, near, far, turned)
    to_up, to_down, to_two, to_across, own = pack(
        (
            halves(0, 0, half) + [(2, chunk, 0, chunk), (3, chunk, 0, chunk), (4, 0, 0, block)],
            halves(1, half, half) + [(2, 3 * chunk, 0, chunk), (3, 3 * chunk, 0, chunk), (4, 0, 0, block)],
            [(2, 2 * chunk, 0, chunk), (3, 2 * chunk, 0, chunk), (4, 0, 0, block)],
            halves(0, 0, F) + halves(1, 0, F) + [(4, 0, 0, block)],
            [(5, 0, 0, 2 * half)],
        ),
        (*parts, wq_old),
        (),
        (WIDTH, WIDTH, WIDTH, WIDTH, 2 * WIDTH),
    )
    across = shift(own, "yl", 1)
    up2 = shift(to_up, "z", 1)
    down2 = shift(to_down, "z", -1)
    two2 = shift(to_two, "z", 2)
    wq_new, query = join(
        (
            (0, 0, 2 * half, "q", 0, 0, 0, 0, 2 * WIDTH),
            (1, 0, 2 * half, "q", 0, -1, 0, 0, 2 * WIDTH),
            (2, 0, 2 * half, "q", 0, 1, 0, 0, 2 * WIDTH),
        ),
        (wq_old, up, down),
        normed,
    )
    across2 = shift(to_across, "yl", 1)

    later = across[F:]
    up3 = shift(later, "z", 1)
    down3 = shift(later, "z", -1)
    page_rows = 2 * half
    wkv_at = page_rows + 2 * chunk
    sorted_pages, to_across3, to_core = sort(
        (near, far, up2, down2, two2, turned, across2),
        [
            (0, 0, 0, 0),
            (1, 0, 0, chunk),
            (2, page_rows, 1, 0),
            (2, page_rows + chunk, 1, chunk),
            (3, page_rows, 3, 0),
            (3, page_rows + chunk, 3, chunk),
            (4, 0, 2, 0),
            (4, chunk, 2, chunk),
        ],
        chunk,
        [
            [(2, 0, F), (2, half, F), (2, wkv_at, block), (3, wkv_at, block), (4, 2 * chunk, block)],
            [
                (5, 0, block),
                (2, wkv_at, block),
                (3, wkv_at, block),
                (4, 2 * chunk, block),
                (6, 4 * F, block),
            ],
        ],
        (across,),
    )
    across3 = shift(to_across3, "yl", 1)
    mine = lax.all_to_all(sorted_pages, "x", split_axis=0, concat_axis=0, tiled=True)
    wq_new, query = join(
        (
            (0, 0, 2 * half, "q", 1, 0, 0, 0, 2 * WIDTH),
            (1, 0, half, "q", 0, 2, 0, 0, WIDTH),
            (1, half, half, "q", 0, 2, 0, WIDTH, WIDTH),
            (2, 0, half, "q", 0, 2, half, 0, WIDTH),
            (2, half, half, "q", 0, 2, half, WIDTH, WIDTH),
            (3, 0, F, "q", 1, -1, 0, 0, WIDTH),
            (3, F, F, "q", 1, -1, 0, WIDTH, WIDTH),
            (3, 2 * F, F, "q", 1, 1, 0, 0, WIDTH),
            (3, 3 * F, F, "q", 1, 1, 0, WIDTH, WIDTH),
        ),
        (across, up2, down2, across2),
        normed,
        (wq_new, query),
    )
    swapped = shift(to_core, "core", 1)

    mine = mine.reshape(-1, WIDTH)
    other = shift(mine, "core", 1)
    swapped2 = shift(across3, "core", 1)
    to_up4, to_down4 = pack(
        ([(0, 0, 0, split)], [(1, split, 0, split)]), (up3, down3), (), (2 * WIDTH, 2 * WIDTH)
    )
    up4 = shift(to_up4, "z", 1)
    down4 = shift(to_down4, "z", -1)
    wq_new, wkv_new, query, fresh = join(
        (
            (0, 0, rest, "q", 1, -1, F, 0, 2 * WIDTH),
            (1, 0, rest, "q", 1, 1, F, 0, 2 * WIDTH),
            (2, 0, F, "q", 1, 2, 0, 0, WIDTH),
            (2, F, F, "q", 1, 2, 0, WIDTH, WIDTH),
            (2, 2 * F, block, "own", 1, -1, 0, 0, WIDTH),
            (2, 2 * F + block, block, "own", 1, 1, 0, 0, WIDTH),
            (2, 2 * F + 2 * block, block, "own", 1, 2, 0, 0, WIDTH),
            (3, 0, block, "own", 0, 0, 0, 0, WIDTH),
            (3, block, block, "own", 0, -1, 0, 0, WIDTH),
            (3, 2 * block, block, "own", 0, 1, 0, 0, WIDTH),
            (3, 3 * block, block, "own", 0, 2, 0, 0, WIDTH),
            (3, 4 * block, block, "own", 1, 0, 0, 0, WIDTH),
        ),
        (up3, down3, across3, to_core),
        normed,
        (wq_new, query),
    )

    spots = ((0, 0), (0, -1), (0, 1), (0, 2), (1, 0))
    spots2 = ((1, -1), (1, 1), (1, 2))
    wq_new, wkv_new, kv_new, context = last(
        (
            *[
                (2, n * block, block, "other", dy, dz, 0, 0, WIDTH)
                for n, (dy, dz) in enumerate(spots)
            ],
            *[
                (3, 2 * F + n * block, block, "other", dy, dz, 0, 0, WIDTH)
                for n, (dy, dz) in enumerate(spots2)
            ],
            (0, 0, split, "q", 1, 2, F, 0, 2 * WIDTH),
            (1, 0, split, "q", 1, 2, F + split, 0, 2 * WIDTH),
        ),
        (up4, down4, swapped, swapped2),
        (mine, other),
        page,
        src,
        lengths,
        normed,
        cosine,
        sine,
        query,
        fresh,
        wq_new,
        wkv_new,
    )
    return (context, kv_new, wq_new, wkv_new)


def solution(mesh):
    torus = Mesh(mesh.devices.reshape(2, 4, 2, 4, 2), ("yl", "z", "yh", "x", "core"))
    return jax.shard_map(
        shards,
        mesh=torus,
        in_specs=(
            P(SECTION, None),
            P(),
            P(SECTION, TENSOR),
            P(TENSOR, SECTION),
            P(SECTION, TENSOR, None, None),
            P(),
            P(),
        ),
        out_specs=(
            P(SECTION, TENSOR),
            P(SECTION, TENSOR, None, None),
            P(None, TENSOR),
            P(None, TENSOR),
        ),
        check_vma=False,
    )
```

```python
import functools

import jax
import jax.numpy as jnp
from jax import lax
from jax.experimental import pallas as pl
from jax.experimental.pallas import tpu as pltpu
from jax.sharding import Mesh
from jax.sharding import PartitionSpec as P

KV_HEADS = 8
HEAD_DIM = 128
WIDTH = 2 * HEAD_DIM
SECTION = ("yl", "z")
TENSOR = ("yh", "x", "core")
EPSILON = 1e-05
ROPE_BASE = 500000.0
VMEM_LIMIT = 10 * 1024 * 1024
LAST_LIMIT = 16 * 1024 * 1024
BUSY = 4 * 10**10

F = 128

ANY = pl.BlockSpec(memory_space=pl.ANY)
HBM = pl.BlockSpec(memory_space=pltpu.HBM)
VM = pl.BlockSpec(memory_space=pltpu.VMEM)
SM = pl.BlockSpec(memory_space=pltpu.SMEM)


def params(limit=VMEM_LIMIT):
    return pltpu.CompilerParams(vmem_limit_bytes=limit)


def cost(flops, nbytes):
    return pl.CostEstimate(flops=flops, bytes_accessed=nbytes, transcendentals=0)


def block_of(dy, dz):
    return lax.rem(lax.axis_index("yl") + dy, 2) * 4 + lax.rem(lax.axis_index("z") + dz + 4, 4)


def source_of(dy, dz):
    gap = lax.axis_index("z") + dz - lax.axis_index("x") + 8
    return lax.rem(lax.axis_index("yl") + dy, 2) * 4 + lax.rem(gap, 4)


def shift(value, axis, by):
    n = lax.axis_size(axis)
    return lax.ppermute(value, axis, [(i, (i + by) % n) for i in range(n)])


def pick_kernel(table_ref, kv_ref, *refs):
    out_refs, src_ref = refs[:2], refs[2]
    picked, spots, spots_s, sems = refs[3:]
    reqs, width = table_ref.shape
    pages = kv_ref.shape[1]
    per_block = pages // reqs
    yl, z = lax.axis_index("yl"), lax.axis_index("z")
    yh, x, core = lax.axis_index("yh"), lax.axis_index("x"), lax.axis_index("core")
    table = table_ref[...]
    owner = table // pages
    local = table % pages
    before = lax.broadcasted_iota(jnp.int32, (width, width), 0)
    after = lax.broadcasted_iota(jnp.int32, (width, width), 1)
    tri = (before < after).astype(jnp.float32)
    mine = owner == yh * 8 + x * 2 + core
    rank = jnp.dot(mine.astype(jnp.float32), tri, preferred_element_type=jnp.float32)
    lanes = lax.broadcasted_iota(jnp.int32, (reqs, 128), 1)
    chosen = jnp.zeros((reqs, 128), jnp.int32)
    for k in range(per_block):
        hit = jnp.where(mine & (rank == k), local, 0)
        chosen = jnp.where(lanes == k, jnp.sum(hit, axis=1, keepdims=True), chosen)
    spots[...] = chosen
    move = pltpu.make_async_copy(spots, spots_s, sems.at[1])
    move.start()
    rows = src_ref.shape[0]
    first = pl.multiple_of((yl * 4 + z) * rows, rows)
    own = table_ref[pl.ds(first, rows), :] // pages
    ranks = jnp.zeros((rows, width), jnp.float32)
    for t in range(16):
        at = (own == t).astype(jnp.float32)
        ranks += at * jnp.dot(at, tri, preferred_element_type=jnp.float32)
    request = lax.broadcasted_iota(jnp.int32, (rows, width), 0)
    place = (own + core) % 2 * 4 + own // 2 % 4
    place = place * 2 + (own // 8 + yl) % 2
    place = (place * rows + request) * per_block
    src_ref[...] = place + ranks.astype(jnp.int32)
    move.wait()
    outs = []
    for n in range(8):
        turn, dz = n // 4, n % 4
        start = (lax.rem(yh + turn, 2) * 4 + lax.rem(z + dz, 4)) * rows

        def body(i, _, n=n, start=start):
            for k in range(per_block):
                picked[(n * rows + i) * per_block + k] = kv_ref[0, spots_s[start + i, k]]
            return 0

        lax.fori_loop(0, rows, body, 0)
        size = rows * per_block
        out = pltpu.make_async_copy(
            picked.at[pl.ds(n * size, size)],
            out_refs[turn].at[pl.ds(dz * size, size)],
            sems.at[2 + n],
        )
        out.start()
        outs.append(out)
    for out in outs:
        out.wait()


def pick(page_table, kv_old):
    pages, page, width = kv_old.shape[1:]
    reqs = page_table.shape[0]
    part = jax.ShapeDtypeStruct((pages // 2, page, width), jnp.bfloat16)
    return pl.pallas_call(
        pick_kernel,
        out_shape=(part, part, jax.ShapeDtypeStruct((reqs // 8, page_table.shape[1]), jnp.int32)),
        in_specs=[VM, VM],
        out_specs=(ANY, ANY, VM),
        scratch_shapes=[
            pltpu.VMEM((pages, page, width), jnp.bfloat16),
            pltpu.VMEM((reqs, 128), jnp.int32),
            pltpu.SMEM((reqs, 128), jnp.int32),
            pltpu.SemaphoreType.DMA((10,)),
        ],
        compiler_params=params(),
        cost_estimate=cost(BUSY, 4 << 20),
    )(page_table, kv_old)


def pack_kernel(copies, sources, outputs, *refs):
    parts, rest = refs[:sources], refs[-2 * outputs - 2 :]
    outs, stages, sem_in, sem_out = rest[:outputs], rest[outputs:-2], rest[-2], rest[-1]
    moves = []
    for n, (i, low, col, rows, o, at) in enumerate(copies):
        move = pltpu.make_async_copy(
            parts[i].at[pl.ds(low, rows), pl.ds(col, outs[o].shape[1])],
            stages[o].at[pl.ds(at, rows)],
            sem_in.at[n],
        )
        move.start()
        moves.append(move)
    sent = []
    for n, (_, _, _, rows, o, at) in enumerate(copies):
        moves[n].wait()
        span = pl.ds(at, rows)
        move = pltpu.make_async_copy(stages[o].at[span], outs[o].at[span], sem_out.at[n])
        move.start()
        sent.append(move)
    for move in sent:
        move.wait()


def pack(layouts, parts, after=(), widths=None):
    widths = widths or (WIDTH,) * len(layouts)
    copies, shapes = [], []
    for o, layout in enumerate(layouts):
        at = 0
        for i, low, col, rows in layout:
            copies.append((i, low, col, rows, o, at))
            at += rows
        shapes.append((at, widths[o]))
    return pl.pallas_call(
        functools.partial(pack_kernel, tuple(copies), len(parts), len(shapes)),
        out_shape=[jax.ShapeDtypeStruct(shape, jnp.bfloat16) for shape in shapes],
        in_specs=[ANY] * (len(parts) + len(after)),
        out_specs=[ANY] * len(shapes),
        scratch_shapes=[pltpu.VMEM(shape, jnp.bfloat16) for shape in shapes]
        + [pltpu.SemaphoreType.DMA((len(copies),)), pltpu.SemaphoreType.DMA((len(copies),))],
        compiler_params=params(),
        cost_estimate=cost(0, sum(a * b * 4 for a, b in shapes)),
    )(*parts, *after)


def sort_kernel(parts, lows, count, copies, *refs):
    ins, out, extras = refs[:parts], refs[-8], refs[-7:-5]
    held, sems, sem_extra = refs[-5], refs[-2], refs[-1]
    stages = refs[-4:-2]
    firsts = []
    for n, (i, low, rows, o, at) in enumerate(copies):
        move = pltpu.make_async_copy(
            ins[i].at[pl.ds(low, rows)], stages[o].at[pl.ds(at, rows)], sem_extra.at[n, 0]
        )
        move.start()
        firsts.append(move)
    moves = []
    for n, (i, low, dz, at) in enumerate(lows):
        move = pltpu.make_async_copy(
            ins[i].at[pl.ds(low, count)], held.at[dz, pl.ds(at, count)], sems.at[n]
        )
        move.start()
        moves.append(move)
    sent = []
    for n, (i, low, rows, o, at) in enumerate(copies):
        firsts[n].wait()
        span = pl.ds(at, rows)
        move = pltpu.make_async_copy(stages[o].at[span], extras[o].at[span], sem_extra.at[n, 1])
        move.start()
        sent.append(move)
    for move in moves:
        move.wait()
    z = lax.axis_index("z") + 4
    moves = []
    for to in range(4):
        move = pltpu.make_async_copy(held.at[lax.rem(z - to, 4)], out.at[to], sems.at[to])
        move.start()
        moves.append(move)
    for move in moves + sent:
        move.wait()


def sort(parts, lows, count, layouts, after=()):
    copies, shapes = [], []
    for o, layout in enumerate(layouts):
        at = 0
        for i, low, rows in layout:
            copies.append((i, low, rows, o, at))
            at += rows
        shapes.append((at, WIDTH))
    return pl.pallas_call(
        functools.partial(sort_kernel, len(parts), tuple(lows), count, tuple(copies)),
        out_shape=[
            jax.ShapeDtypeStruct((4, 2 * count, WIDTH), jnp.bfloat16),
            *[jax.ShapeDtypeStruct(shape, jnp.bfloat16) for shape in shapes],
        ],
        in_specs=[ANY] * (len(parts) + len(after)),
        out_specs=[ANY] * 3,
        scratch_shapes=[
            pltpu.VMEM((4, 2 * count, WIDTH), jnp.bfloat16),
            *[pltpu.VMEM(shape, jnp.bfloat16) for shape in shapes],
            pltpu.SemaphoreType.DMA((len(lows),)),
            pltpu.SemaphoreType.DMA((len(copies), 2)),
        ],
        compiler_params=params(),
        cost_estimate=cost(0, 8 << 20),
    )(*parts, *after)


def land(plan, buffers, loads, wholes, normed_ref, query, fresh, sems):
    outs, waited = [], set()
    query = list(query)
    for n, (i, low, rows, kind, dy, dz, at, col, width) in enumerate(plan):
        if i not in waited:
            loads[i].wait()
            waited.add(i)
        if kind == "q":
            start = pl.multiple_of(block_of(dy, dz) * 1024 + at, 128)
            whole = wholes[0].at[pl.ds(start, rows), pl.ds(col, width)]
        else:
            core = lax.axis_index("core")
            half = core if kind == "own" else 1 - core
            start = pl.multiple_of((source_of(dy, dz) * 2 + half) * 512, 512)
            whole = wholes[1].at[pl.ds(start, rows)]
        out = pltpu.make_async_copy(buffers[i].at[pl.ds(low, rows)], whole, sems.at[n])
        out.start()
        outs.append(out)
        normed = normed_ref[:, pl.ds(start, rows)]
        for c in range(0, width, WIDTH):
            term = jnp.dot(
                normed,
                buffers[i][low : low + rows, c : c + WIDTH],
                preferred_element_type=jnp.float32,
            )
            if kind == "q":
                query[(col + c) // WIDTH] += term
            else:
                fresh += term
    return query, fresh, outs


def join_kernel(plan, count, state, *refs):
    parts, normed_ref = refs[:count], refs[count]
    rest = refs[count + 1 :]
    wholes_n = 2 if any(item[3] != "q" for item in plan) else 1
    rows, columns = normed_ref.shape[0], 2 * WIDTH
    if state:
        query_in, rest = rest[0], rest[2:]
        query = [query_in[:, :WIDTH], query_in[:, WIDTH:]]
    else:
        query = [jnp.zeros((rows, WIDTH), jnp.float32)] * 2
    wholes, rest = rest[:wholes_n], rest[wholes_n:]
    query_ref, rest = rest[0], rest[1:]
    if wholes_n == 2:
        fresh_ref, rest = rest[0], rest[1:]
    buffers, sem_in, sem_out = rest[:count], rest[count], rest[count + 1]
    loads = []
    for i in range(count):
        load = pltpu.make_async_copy(parts[i], buffers[i], sem_in.at[i])
        load.start()
        loads.append(load)
    fresh = jnp.zeros((rows, WIDTH), jnp.float32)
    query, fresh, outs = land(plan, buffers, loads, wholes, normed_ref, query, fresh, sem_out)
    query_ref[:, :WIDTH] = query[0]
    query_ref[:, WIDTH:] = query[1]
    if wholes_n == 2:
        fresh_ref[...] = fresh
    for out in outs:
        out.wait()


def join(plan, parts, normed, state=None, after=(), busy=BUSY):
    rows, depth = normed.shape
    kv = any(item[3] != "q" for item in plan)
    args = [*parts, normed]
    in_specs = [ANY] * len(parts) + [VM]
    aliases = {}
    if state is not None:
        whole, query = state
        args += [query, whole]
        in_specs += [VM, HBM]
        aliases = {len(parts) + 2: 0}
    out_shape = [jax.ShapeDtypeStruct((depth, 2 * WIDTH), jnp.bfloat16)]
    out_specs = [HBM]
    if kv:
        out_shape.append(jax.ShapeDtypeStruct((depth, WIDTH), jnp.bfloat16))
        out_specs.append(HBM)
    out_shape.append(jax.ShapeDtypeStruct((rows, 2 * WIDTH), jnp.float32))
    out_specs.append(VM)
    if kv:
        out_shape.append(jax.ShapeDtypeStruct((rows, WIDTH), jnp.float32))
        out_specs.append(VM)
    nbytes = sum(part.size * 4 for part in parts)
    return pl.pallas_call(
        functools.partial(join_kernel, plan, len(parts), state is not None),
        out_shape=out_shape,
        in_specs=in_specs,
        out_specs=out_specs,
        input_output_aliases=aliases,
        scratch_shapes=[pltpu.VMEM(part.shape, jnp.bfloat16) for part in parts]
        + [pltpu.SemaphoreType.DMA((len(parts),)), pltpu.SemaphoreType.DMA((len(plan),))],
        compiler_params=params(),
        cost_estimate=cost(busy, nbytes),
    )(*args)


def turn(value, cosine, sine):
    return value * cosine + pltpu.roll(value, HEAD_DIM // 2, 1) * sine


def last_kernel(plan, count, page, *refs):
    parts, (mine_ref, other_ref) = refs[:count], refs[count : count + 2]
    rest = refs[count + 2 :]
    src_ref, lengths_ref, normed_ref, cos_ref, sin_ref, query_ref, fresh_ref = rest[:7]
    rest = rest[9:]
    wq_ref, wkv_ref, cache_ref, context_ref = rest[:4]
    rest = rest[4:]
    buffers, rest = rest[:count], rest[count:]
    built, heads, mixed, sem_in, sem_out, sem_cache = rest
    rows, slots = built.shape[:2]
    loads = []
    for i in range(count):
        load = pltpu.make_async_copy(parts[i], buffers[i], sem_in.at[i])
        load.start()
        loads.append(load)
    total = mine_ref.shape[0] // page
    for r in range(rows):

        def body(j, _, r=r):
            for n in range(8):
                at = pl.multiple_of((j * 8 + n) * page, page)
                place = src_ref[r, j * 8 + n]
                low = pl.multiple_of(place % total * page, page)
                near = mine_ref[pl.ds(low, page), :]
                far = other_ref[pl.ds(low, page), :]
                built[r, pl.ds(at, page), :] = jnp.where(place < total, near, far)
            return 0

        lax.fori_loop(0, slots // page // 8, body, 0)
    query = [query_ref[:, :WIDTH], query_ref[:, WIDTH:]]
    query, fresh, outs = land(
        plan, buffers, loads, (wq_ref, wkv_ref), normed_ref, query, fresh_ref[...], sem_out
    )
    cosine, sine = cos_ref[...], sin_ref[...]
    fresh = jnp.concatenate(
        [turn(fresh[:, :HEAD_DIM], cosine, sine), fresh[:, HEAD_DIM:]], axis=1
    )
    count_q = 2 * WIDTH // HEAD_DIM
    heads[...] = jnp.zeros_like(heads)
    for h in range(count_q):
        value = query[h * HEAD_DIM // WIDTH]
        low = h * HEAD_DIM % WIDTH
        heads[:, h, :] = turn(value[:, low : low + HEAD_DIM], cosine, sine)
    first = (lax.axis_index("yl") * 4 + lax.axis_index("z")) * rows
    for r in range(rows):
        length = lengths_ref[first + r]
        at = pl.multiple_of(length // page * page, page)
        old = built[r, pl.ds(at, page), :]
        line = lax.broadcasted_iota(jnp.int32, old.shape, 0)
        new = jnp.broadcast_to(fresh[r : r + 1, :], old.shape)
        built[r, pl.ds(at, page), :] = jnp.where(
            line == length % page, new, old.astype(jnp.float32)
        ).astype(jnp.bfloat16)
        out = pltpu.make_async_copy(built.at[r], cache_ref.at[r, 0], sem_cache.at[r])
        out.start()
        outs.append(out)
    for r in range(rows):
        length = lengths_ref[first + r]
        scores = lax.dot_general(
            heads[r].astype(jnp.bfloat16),
            built[r, :, :HEAD_DIM],
            (((1,), (1,)), ((), ())),
            preferred_element_type=jnp.float32,
        ) * HEAD_DIM ** (-0.5)
        seen = lax.broadcasted_iota(jnp.int32, scores.shape, 1) <= length
        peak = jnp.max(jnp.where(seen, scores, -jnp.inf), axis=1, keepdims=True)
        weights = jnp.where(seen, jnp.exp(scores - peak), 0.0)
        probs = (weights / jnp.sum(weights, axis=1, keepdims=True)).astype(jnp.bfloat16)
        result = jnp.dot(probs, built[r, :, HEAD_DIM:], preferred_element_type=jnp.float32)
        for h in range(count_q):
            mixed[r : r + 1, h * HEAD_DIM : (h + 1) * HEAD_DIM] = result[h : h + 1, :]
    context_ref[...] = mixed[...].astype(jnp.bfloat16)
    for out in outs:
        out.wait()


def last(plan, parts, pools, page, src, lengths, normed, cosine, sine, query, fresh, wq_new, wkv_new):
    rows = normed.shape[0]
    slots = src.shape[1] * page
    args = [*parts, *pools, src, lengths, normed, cosine, sine, query, fresh, wq_new, wkv_new]
    lead = len(parts) + len(pools)
    return pl.pallas_call(
        functools.partial(last_kernel, plan, len(parts), page),
        out_shape=[
            jax.ShapeDtypeStruct(wq_new.shape, jnp.bfloat16),
            jax.ShapeDtypeStruct(wkv_new.shape, jnp.bfloat16),
            jax.ShapeDtypeStruct((rows, 1, slots, WIDTH), jnp.bfloat16),
            jax.ShapeDtypeStruct(query.shape, jnp.bfloat16),
        ],
        in_specs=[ANY] * len(parts) + [VM, VM, SM, SM, VM, VM, VM, VM, VM, HBM, HBM],
        out_specs=[HBM, HBM, HBM, VM],
        input_output_aliases={lead + 7: 0, lead + 8: 1},
        scratch_shapes=[pltpu.VMEM(part.shape, jnp.bfloat16) for part in parts]
        + [
            pltpu.VMEM((rows, slots, WIDTH), jnp.bfloat16),
            pltpu.VMEM((rows, 8, HEAD_DIM), jnp.float32),
            pltpu.VMEM(query.shape, jnp.float32),
            pltpu.SemaphoreType.DMA((len(parts),)),
            pltpu.SemaphoreType.DMA((len(plan),)),
            pltpu.SemaphoreType.DMA((rows,)),
        ],
        compiler_params=params(LAST_LIMIT),
        cost_estimate=cost(64 << 20, 16 << 20),
    )(*args)


def halves(part, low, rows):
    return [(part, low, 0, rows), (part, low, WIDTH, rows)]


def shards(hidden_state, norm_gain, wq_old, wkv_old, kv_old, page_table, lengths):
    rows = hidden_state.shape[0]
    page = kv_old.shape[2]
    half = wq_old.shape[0] // 2
    rest = wq_old.shape[0] - F
    split = rest // 256 * 128

    pairs = []
    for yl in range(2):
        for z in range(4):
            for yh in range(2):
                for x in range(4):
                    here = ((yl * 4 + z) * 2 + yh) * 4 + x
                    pairs.append((here, ((yh * 4 + (z + x) % 4) * 2 + yl) * 4 + x))
    moved = lax.ppermute(wkv_old, ("yl", "z", "yh", "x"), pairs)
    (held,) = pack(([(0, 0, 0, wq_old.shape[0])],), (wq_old,), (moved,), (2 * WIDTH,))
    up = shift(held, "z", 1)
    down = shift(held, "z", -1)
    picked = pick(page_table, kv_old)
    src = picked[2]
    near, far = [
        lax.ppermute(
            picked[flip].reshape(-1, WIDTH),
            ("yl", "yh"),
            [(a * 2 + b, (b ^ flip) * 2 + a) for a in range(2) for b in range(2)],
        )
        for flip in range(2)
    ]
    turned = lax.ppermute(
        moved, ("z", "x"), [(z * 4 + x, z * 4 + (z - x) % 4) for z in range(4) for x in range(4)]
    )

    my_lengths = lax.dynamic_slice_in_dim(lengths, lax.axis_index(SECTION) * rows, rows, 0)
    widened = hidden_state.astype(jnp.float32)
    scale = lax.rsqrt(jnp.mean(widened * widened, axis=1, keepdims=True) + EPSILON)
    normed = (widened * scale * norm_gain[None, :]).astype(jnp.bfloat16)
    spread = HEAD_DIM // 2
    frequency = ROPE_BASE ** (-(jnp.arange(spread, dtype=jnp.float32) * 2.0 / HEAD_DIM))
    angles = my_lengths.astype(jnp.float32)[:, None] * frequency[None, :]
    cosine, sine = jnp.cos(angles), jnp.sin(angles)
    cosine = jnp.concatenate([cosine, cosine], axis=1)
    sine = jnp.concatenate([-sine, sine], axis=1)

    chunk = near.shape[0] // 4
    block = turned.shape[0]
    parts = (up, down, near, far, turned)
    to_up, to_down, to_two, to_across, own = pack(
        (
            halves(0, 0, half) + [(2, chunk, 0, chunk), (3, chunk, 0, chunk), (4, 0, 0, block)],
            halves(1, half, half) + [(2, 3 * chunk, 0, chunk), (3, 3 * chunk, 0, chunk), (4, 0, 0, block)],
            [(2, 2 * chunk, 0, chunk), (3, 2 * chunk, 0, chunk), (4, 0, 0, block)],
            halves(0, 0, F) + halves(1, 0, F) + [(4, 0, 0, block)],
            [(5, 0, 0, 2 * half)],
        ),
        (*parts, wq_old),
        (),
        (WIDTH, WIDTH, WIDTH, WIDTH, 2 * WIDTH),
    )
    across = shift(own, "yl", 1)
    up2 = shift(to_up, "z", 1)
    down2 = shift(to_down, "z", -1)
    two2 = shift(to_two, "z", 2)
    wq_new, query = join(
        (
            (0, 0, 2 * half, "q", 0, 0, 0, 0, 2 * WIDTH),
            (1, 0, 2 * half, "q", 0, -1, 0, 0, 2 * WIDTH),
            (2, 0, 2 * half, "q", 0, 1, 0, 0, 2 * WIDTH),
        ),
        (wq_old, up, down),
        normed,
    )
    across2 = shift(to_across, "yl", 1)

    later = across[F:]
    up3 = shift(later, "z", 1)
    down3 = shift(later, "z", -1)
    page_rows = 2 * half
    wkv_at = page_rows + 2 * chunk
    sorted_pages, to_across3, to_core = sort(
        (near, far, up2, down2, two2, turned, across2),
        [
            (0, 0, 0, 0),
            (1, 0, 0, chunk),
            (2, page_rows, 1, 0),
            (2, page_rows + chunk, 1, chunk),
            (3, page_rows, 3, 0),
            (3, page_rows + chunk, 3, chunk),
            (4, 0, 2, 0),
            (4, chunk, 2, chunk),
        ],
        chunk,
        [
            [(2, 0, F), (2, half, F), (2, wkv_at, block), (3, wkv_at, block), (4, 2 * chunk, block)],
            [
                (5, 0, block),
                (2, wkv_at, block),
                (3, wkv_at, block),
                (4, 2 * chunk, block),
                (6, 4 * F, block),
            ],
        ],
        (across,),
    )
    across3 = shift(to_across3, "yl", 1)
    mine = lax.all_to_all(sorted_pages, "x", split_axis=0, concat_axis=0, tiled=True)
    wq_new, query = join(
        (
            (0, 0, 2 * half, "q", 1, 0, 0, 0, 2 * WIDTH),
            (1, 0, half, "q", 0, 2, 0, 0, WIDTH),
            (1, half, half, "q", 0, 2, 0, WIDTH, WIDTH),
            (2, 0, half, "q", 0, 2, half, 0, WIDTH),
            (2, half, half, "q", 0, 2, half, WIDTH, WIDTH),
            (3, 0, F, "q", 1, -1, 0, 0, WIDTH),
            (3, F, F, "q", 1, -1, 0, WIDTH, WIDTH),
            (3, 2 * F, F, "q", 1, 1, 0, 0, WIDTH),
            (3, 3 * F, F, "q", 1, 1, 0, WIDTH, WIDTH),
        ),
        (across, up2, down2, across2),
        normed,
        (wq_new, query),
    )
    swapped = shift(to_core, "core", 1)

    mine = mine.reshape(-1, WIDTH)
    other = shift(mine, "core", 1)
    swapped2 = shift(across3, "core", 1)
    to_up4, to_down4 = pack(
        ([(0, 0, 0, split)], [(1, split, 0, rest - split)]), (up3, down3), (), (2 * WIDTH, 2 * WIDTH)
    )
    up4 = shift(to_up4, "z", 1)
    down4 = shift(to_down4, "z", -1)
    wq_new, wkv_new, query, fresh = join(
        (
            (0, 0, rest, "q", 1, -1, F, 0, 2 * WIDTH),
            (1, 0, rest, "q", 1, 1, F, 0, 2 * WIDTH),
            (2, 0, F, "q", 1, 2, 0, 0, WIDTH),
            (2, F, F, "q", 1, 2, 0, WIDTH, WIDTH),
            (2, 2 * F, block, "own", 1, -1, 0, 0, WIDTH),
            (2, 2 * F + block, block, "own", 1, 1, 0, 0, WIDTH),
            (2, 2 * F + 2 * block, block, "own", 1, 2, 0, 0, WIDTH),
            (3, 0, block, "own", 0, 0, 0, 0, WIDTH),
            (3, block, block, "own", 0, -1, 0, 0, WIDTH),
            (3, 2 * block, block, "own", 0, 1, 0, 0, WIDTH),
            (3, 3 * block, block, "own", 0, 2, 0, 0, WIDTH),
            (3, 4 * block, block, "own", 1, 0, 0, 0, WIDTH),
        ),
        (up3, down3, across3, to_core),
        normed,
        (wq_new, query),
    )

    spots = ((0, 0), (0, -1), (0, 1), (0, 2), (1, 0))
    spots2 = ((1, -1), (1, 1), (1, 2))
    wq_new, wkv_new, kv_new, context = last(
        (
            *[
                (2, n * block, block, "other", dy, dz, 0, 0, WIDTH)
                for n, (dy, dz) in enumerate(spots)
            ],
            *[
                (3, 2 * F + n * block, block, "other", dy, dz, 0, 0, WIDTH)
                for n, (dy, dz) in enumerate(spots2)
            ],
            (0, 0, split, "q", 1, 2, F, 0, 2 * WIDTH),
            (1, 0, rest - split, "q", 1, 2, F + split, 0, 2 * WIDTH),
        ),
        (up4, down4, swapped, swapped2),
        (mine, other),
        page,
        src,
        lengths,
        normed,
        cosine,
        sine,
        query,
        fresh,
        wq_new,
        wkv_new,
    )
    return (context, kv_new, wq_new, wkv_new)


def solution(mesh):
    torus = Mesh(mesh.devices.reshape(2, 4, 2, 4, 2), ("yl", "z", "yh", "x", "core"))
    return jax.shard_map(
        shards,
        mesh=torus,
        in_specs=(
            P(SECTION, None),
            P(),
            P(SECTION, TENSOR),
            P(TENSOR, SECTION),
            P(SECTION, TENSOR, None, None),
            P(),
            P(),
        ),
        out_specs=(
            P(SECTION, TENSOR),
            P(SECTION, TENSOR, None, None),
            P(None, TENSOR),
            P(None, TENSOR),
        ),
        check_vma=False,
    )
```

```python
import functools

import jax
import jax.numpy as jnp
from jax import lax
from jax.experimental import pallas as pl
from jax.experimental.pallas import tpu as pltpu
from jax.sharding import Mesh
from jax.sharding import PartitionSpec as P

KV_HEADS = 8
HEAD_DIM = 128
WIDTH = 2 * HEAD_DIM
SECTION = ("yl", "z")
TENSOR = ("yh", "x", "core")
EPSILON = 1e-05
ROPE_BASE = 500000.0
VMEM_LIMIT = 10 * 1024 * 1024
LAST_LIMIT = 16 * 1024 * 1024
BUSY = 4 * 10**10

F = 256

ANY = pl.BlockSpec(memory_space=pl.ANY)
HBM = pl.BlockSpec(memory_space=pltpu.HBM)
VM = pl.BlockSpec(memory_space=pltpu.VMEM)
SM = pl.BlockSpec(memory_space=pltpu.SMEM)


def params(limit=VMEM_LIMIT):
    return pltpu.CompilerParams(vmem_limit_bytes=limit)


def cost(flops, nbytes):
    return pl.CostEstimate(flops=flops, bytes_accessed=nbytes, transcendentals=0)


def block_of(dy, dz):
    return lax.rem(lax.axis_index("yl") + dy, 2) * 4 + lax.rem(lax.axis_index("z") + dz + 4, 4)


def source_of(dy, dz):
    gap = lax.axis_index("z") + dz - lax.axis_index("x") + 8
    return lax.rem(lax.axis_index("yl") + dy, 2) * 4 + lax.rem(gap, 4)


def shift(value, axis, by):
    n = lax.axis_size(axis)
    return lax.ppermute(value, axis, [(i, (i + by) % n) for i in range(n)])


def pick_kernel(table_ref, kv_ref, *refs):
    out_refs, src_ref = refs[:2], refs[2]
    picked, spots, spots_s, sems = refs[3:]
    reqs, width = table_ref.shape
    pages = kv_ref.shape[1]
    per_block = pages // reqs
    yl, z = lax.axis_index("yl"), lax.axis_index("z")
    yh, x, core = lax.axis_index("yh"), lax.axis_index("x"), lax.axis_index("core")
    table = table_ref[...]
    owner = table // pages
    local = table % pages
    before = lax.broadcasted_iota(jnp.int32, (width, width), 0)
    after = lax.broadcasted_iota(jnp.int32, (width, width), 1)
    tri = (before < after).astype(jnp.float32)
    mine = owner == yh * 8 + x * 2 + core
    rank = jnp.dot(mine.astype(jnp.float32), tri, preferred_element_type=jnp.float32)
    lanes = lax.broadcasted_iota(jnp.int32, (reqs, 128), 1)
    chosen = jnp.zeros((reqs, 128), jnp.int32)
    for k in range(per_block):
        hit = jnp.where(mine & (rank == k), local, 0)
        chosen = jnp.where(lanes == k, jnp.sum(hit, axis=1, keepdims=True), chosen)
    spots[...] = chosen
    move = pltpu.make_async_copy(spots, spots_s, sems.at[1])
    move.start()
    rows = src_ref.shape[0]
    first = pl.multiple_of((yl * 4 + z) * rows, rows)
    own = table_ref[pl.ds(first, rows), :] // pages
    ranks = jnp.zeros((rows, width), jnp.float32)
    for t in range(16):
        at = (own == t).astype(jnp.float32)
        ranks += at * jnp.dot(at, tri, preferred_element_type=jnp.float32)
    request = lax.broadcasted_iota(jnp.int32, (rows, width), 0)
    place = (own + core) % 2 * 4 + own // 2 % 4
    place = place * 2 + (own // 8 + yl) % 2
    place = (place * rows + request) * per_block
    src_ref[...] = place + ranks.astype(jnp.int32)
    move.wait()
    outs = []
    for n in range(8):
        turn, dz = n // 4, n % 4
        start = (lax.rem(yh + turn, 2) * 4 + lax.rem(z + dz, 4)) * rows

        def body(i, _, n=n, start=start):
            for k in range(per_block):
                picked[(n * rows + i) * per_block + k] = kv_ref[0, spots_s[start + i, k]]
            return 0

        lax.fori_loop(0, rows, body, 0)
        size = rows * per_block
        out = pltpu.make_async_copy(
            picked.at[pl.ds(n * size, size)],
            out_refs[turn].at[pl.ds(dz * size, size)],
            sems.at[2 + n],
        )
        out.start()
        outs.append(out)
    for out in outs:
        out.wait()


def pick(page_table, kv_old):
    pages, page, width = kv_old.shape[1:]
    reqs = page_table.shape[0]
    part = jax.ShapeDtypeStruct((pages // 2, page, width), jnp.bfloat16)
    return pl.pallas_call(
        pick_kernel,
        out_shape=(part, part, jax.ShapeDtypeStruct((reqs // 8, page_table.shape[1]), jnp.int32)),
        in_specs=[VM, VM],
        out_specs=(ANY, ANY, VM),
        scratch_shapes=[
            pltpu.VMEM((pages, page, width), jnp.bfloat16),
            pltpu.VMEM((reqs, 128), jnp.int32),
            pltpu.SMEM((reqs, 128), jnp.int32),
            pltpu.SemaphoreType.DMA((10,)),
        ],
        compiler_params=params(),
        cost_estimate=cost(BUSY, 4 << 20),
    )(page_table, kv_old)


def pack_kernel(copies, sources, outputs, *refs):
    parts, rest = refs[:sources], refs[-2 * outputs - 2 :]
    outs, stages, sem_in, sem_out = rest[:outputs], rest[outputs:-2], rest[-2], rest[-1]
    moves = []
    for n, (i, low, col, rows, o, at) in enumerate(copies):
        move = pltpu.make_async_copy(
            parts[i].at[pl.ds(low, rows), pl.ds(col, outs[o].shape[1])],
            stages[o].at[pl.ds(at, rows)],
            sem_in.at[n],
        )
        move.start()
        moves.append(move)
    sent = []
    for n, (_, _, _, rows, o, at) in enumerate(copies):
        moves[n].wait()
        span = pl.ds(at, rows)
        move = pltpu.make_async_copy(stages[o].at[span], outs[o].at[span], sem_out.at[n])
        move.start()
        sent.append(move)
    for move in sent:
        move.wait()


def pack(layouts, parts, after=(), widths=None):
    widths = widths or (WIDTH,) * len(layouts)
    copies, shapes = [], []
    for o, layout in enumerate(layouts):
        at = 0
        for i, low, col, rows in layout:
            copies.append((i, low, col, rows, o, at))
            at += rows
        shapes.append((at, widths[o]))
    return pl.pallas_call(
        functools.partial(pack_kernel, tuple(copies), len(parts), len(shapes)),
        out_shape=[jax.ShapeDtypeStruct(shape, jnp.bfloat16) for shape in shapes],
        in_specs=[ANY] * (len(parts) + len(after)),
        out_specs=[ANY] * len(shapes),
        scratch_shapes=[pltpu.VMEM(shape, jnp.bfloat16) for shape in shapes]
        + [pltpu.SemaphoreType.DMA((len(copies),)), pltpu.SemaphoreType.DMA((len(copies),))],
        compiler_params=params(),
        cost_estimate=cost(0, sum(a * b * 4 for a, b in shapes)),
    )(*parts, *after)


def sort_kernel(parts, lows, count, copies, *refs):
    ins, out, extras = refs[:parts], refs[-8], refs[-7:-5]
    held, sems, sem_extra = refs[-5], refs[-2], refs[-1]
    stages = refs[-4:-2]
    firsts = []
    for n, (i, low, rows, o, at) in enumerate(copies):
        move = pltpu.make_async_copy(
            ins[i].at[pl.ds(low, rows)], stages[o].at[pl.ds(at, rows)], sem_extra.at[n, 0]
        )
        move.start()
        firsts.append(move)
    moves = []
    for n, (i, low, dz, at) in enumerate(lows):
        move = pltpu.make_async_copy(
            ins[i].at[pl.ds(low, count)], held.at[dz, pl.ds(at, count)], sems.at[n]
        )
        move.start()
        moves.append(move)
    sent = []
    for n, (i, low, rows, o, at) in enumerate(copies):
        firsts[n].wait()
        span = pl.ds(at, rows)
        move = pltpu.make_async_copy(stages[o].at[span], extras[o].at[span], sem_extra.at[n, 1])
        move.start()
        sent.append(move)
    for move in moves:
        move.wait()
    z = lax.axis_index("z") + 4
    moves = []
    for to in range(4):
        move = pltpu.make_async_copy(held.at[lax.rem(z - to, 4)], out.at[to], sems.at[to])
        move.start()
        moves.append(move)
    for move in moves + sent:
        move.wait()


def sort(parts, lows, count, layouts, after=()):
    copies, shapes = [], []
    for o, layout in enumerate(layouts):
        at = 0
        for i, low, rows in layout:
            copies.append((i, low, rows, o, at))
            at += rows
        shapes.append((at, WIDTH))
    return pl.pallas_call(
        functools.partial(sort_kernel, len(parts), tuple(lows), count, tuple(copies)),
        out_shape=[
            jax.ShapeDtypeStruct((4, 2 * count, WIDTH), jnp.bfloat16),
            *[jax.ShapeDtypeStruct(shape, jnp.bfloat16) for shape in shapes],
        ],
        in_specs=[ANY] * (len(parts) + len(after)),
        out_specs=[ANY] * 3,
        scratch_shapes=[
            pltpu.VMEM((4, 2 * count, WIDTH), jnp.bfloat16),
            *[pltpu.VMEM(shape, jnp.bfloat16) for shape in shapes],
            pltpu.SemaphoreType.DMA((len(lows),)),
            pltpu.SemaphoreType.DMA((len(copies), 2)),
        ],
        compiler_params=params(),
        cost_estimate=cost(0, 8 << 20),
    )(*parts, *after)


def land(plan, buffers, loads, wholes, normed_ref, query, fresh, sems):
    outs, waited = [], set()
    query = list(query)
    for n, (i, low, rows, kind, dy, dz, at, col, width) in enumerate(plan):
        if i not in waited:
            loads[i].wait()
            waited.add(i)
        if kind == "q":
            start = pl.multiple_of(block_of(dy, dz) * 1024 + at, 128)
            whole = wholes[0].at[pl.ds(start, rows), pl.ds(col, width)]
        else:
            core = lax.axis_index("core")
            half = core if kind == "own" else 1 - core
            start = pl.multiple_of((source_of(dy, dz) * 2 + half) * 512, 512)
            whole = wholes[1].at[pl.ds(start, rows)]
        out = pltpu.make_async_copy(buffers[i].at[pl.ds(low, rows)], whole, sems.at[n])
        out.start()
        outs.append(out)
        normed = normed_ref[:, pl.ds(start, rows)]
        for c in range(0, width, WIDTH):
            term = jnp.dot(
                normed,
                buffers[i][low : low + rows, c : c + WIDTH],
                preferred_element_type=jnp.float32,
            )
            if kind == "q":
                query[(col + c) // WIDTH] += term
            else:
                fresh += term
    return query, fresh, outs


def join_kernel(plan, count, state, *refs):
    parts, normed_ref = refs[:count], refs[count]
    rest = refs[count + 1 :]
    wholes_n = 2 if any(item[3] != "q" for item in plan) else 1
    rows, columns = normed_ref.shape[0], 2 * WIDTH
    if state:
        query_in, rest = rest[0], rest[2:]
        query = [query_in[:, :WIDTH], query_in[:, WIDTH:]]
    else:
        query = [jnp.zeros((rows, WIDTH), jnp.float32)] * 2
    wholes, rest = rest[:wholes_n], rest[wholes_n:]
    query_ref, rest = rest[0], rest[1:]
    if wholes_n == 2:
        fresh_ref, rest = rest[0], rest[1:]
    buffers, sem_in, sem_out = rest[:count], rest[count], rest[count + 1]
    loads = []
    for i in range(count):
        load = pltpu.make_async_copy(parts[i], buffers[i], sem_in.at[i])
        load.start()
        loads.append(load)
    fresh = jnp.zeros((rows, WIDTH), jnp.float32)
    query, fresh, outs = land(plan, buffers, loads, wholes, normed_ref, query, fresh, sem_out)
    query_ref[:, :WIDTH] = query[0]
    query_ref[:, WIDTH:] = query[1]
    if wholes_n == 2:
        fresh_ref[...] = fresh
    for out in outs:
        out.wait()


def join(plan, parts, normed, state=None, after=(), busy=BUSY):
    rows, depth = normed.shape
    kv = any(item[3] != "q" for item in plan)
    args = [*parts, normed]
    in_specs = [ANY] * len(parts) + [VM]
    aliases = {}
    if state is not None:
        whole, query = state
        args += [query, whole]
        in_specs += [VM, HBM]
        aliases = {len(parts) + 2: 0}
    out_shape = [jax.ShapeDtypeStruct((depth, 2 * WIDTH), jnp.bfloat16)]
    out_specs = [HBM]
    if kv:
        out_shape.append(jax.ShapeDtypeStruct((depth, WIDTH), jnp.bfloat16))
        out_specs.append(HBM)
    out_shape.append(jax.ShapeDtypeStruct((rows, 2 * WIDTH), jnp.float32))
    out_specs.append(VM)
    if kv:
        out_shape.append(jax.ShapeDtypeStruct((rows, WIDTH), jnp.float32))
        out_specs.append(VM)
    nbytes = sum(part.size * 4 for part in parts)
    return pl.pallas_call(
        functools.partial(join_kernel, plan, len(parts), state is not None),
        out_shape=out_shape,
        in_specs=in_specs,
        out_specs=out_specs,
        input_output_aliases=aliases,
        scratch_shapes=[pltpu.VMEM(part.shape, jnp.bfloat16) for part in parts]
        + [pltpu.SemaphoreType.DMA((len(parts),)), pltpu.SemaphoreType.DMA((len(plan),))],
        compiler_params=params(),
        cost_estimate=cost(busy, nbytes),
    )(*args)


def turn(value, cosine, sine):
    return value * cosine + pltpu.roll(value, HEAD_DIM // 2, 1) * sine


def last_kernel(plan, count, page, *refs):
    parts, (mine_ref, other_ref) = refs[:count], refs[count : count + 2]
    rest = refs[count + 2 :]
    src_ref, lengths_ref, normed_ref, cos_ref, sin_ref, query_ref, fresh_ref = rest[:7]
    rest = rest[9:]
    wq_ref, wkv_ref, cache_ref, context_ref = rest[:4]
    rest = rest[4:]
    buffers, rest = rest[:count], rest[count:]
    built, heads, mixed, sem_in, sem_out, sem_cache = rest
    rows, slots = built.shape[:2]
    loads = []
    for i in range(count):
        load = pltpu.make_async_copy(parts[i], buffers[i], sem_in.at[i])
        load.start()
        loads.append(load)
    total = mine_ref.shape[0] // page
    for r in range(rows):

        def body(j, _, r=r):
            for n in range(16):
                at = pl.multiple_of((j * 16 + n) * page, page)
                place = src_ref[r, j * 16 + n]
                low = pl.multiple_of(place % total * page, page)
                near = mine_ref[pl.ds(low, page), :]
                far = other_ref[pl.ds(low, page), :]
                built[r, pl.ds(at, page), :] = jnp.where(place < total, near, far)
            return 0

        lax.fori_loop(0, slots // page // 16, body, 0)
    query = [query_ref[:, :WIDTH], query_ref[:, WIDTH:]]
    query, fresh, outs = land(
        plan, buffers, loads, (wq_ref, wkv_ref), normed_ref, query, fresh_ref[...], sem_out
    )
    cosine, sine = cos_ref[...], sin_ref[...]
    fresh = jnp.concatenate(
        [turn(fresh[:, :HEAD_DIM], cosine, sine), fresh[:, HEAD_DIM:]], axis=1
    )
    count_q = 2 * WIDTH // HEAD_DIM
    heads[...] = jnp.zeros_like(heads)
    for h in range(count_q):
        value = query[h * HEAD_DIM // WIDTH]
        low = h * HEAD_DIM % WIDTH
        heads[:, h, :] = turn(value[:, low : low + HEAD_DIM], cosine, sine)
    first = (lax.axis_index("yl") * 4 + lax.axis_index("z")) * rows
    for r in range(rows):
        length = lengths_ref[first + r]
        at = pl.multiple_of(length // page * page, page)
        old = built[r, pl.ds(at, page), :]
        line = lax.broadcasted_iota(jnp.int32, old.shape, 0)
        new = jnp.broadcast_to(fresh[r : r + 1, :], old.shape)
        built[r, pl.ds(at, page), :] = jnp.where(
            line == length % page, new, old.astype(jnp.float32)
        ).astype(jnp.bfloat16)
        out = pltpu.make_async_copy(built.at[r], cache_ref.at[r, 0], sem_cache.at[r])
        out.start()
        outs.append(out)
    for r in range(rows):
        length = lengths_ref[first + r]
        scores = lax.dot_general(
            heads[r].astype(jnp.bfloat16),
            built[r, :, :HEAD_DIM],
            (((1,), (1,)), ((), ())),
            preferred_element_type=jnp.float32,
        ) * HEAD_DIM ** (-0.5)
        seen = lax.broadcasted_iota(jnp.int32, scores.shape, 1) <= length
        peak = jnp.max(jnp.where(seen, scores, -jnp.inf), axis=1, keepdims=True)
        weights = jnp.where(seen, jnp.exp(scores - peak), 0.0)
        probs = (weights / jnp.sum(weights, axis=1, keepdims=True)).astype(jnp.bfloat16)
        result = jnp.dot(probs, built[r, :, HEAD_DIM:], preferred_element_type=jnp.float32)
        for h in range(count_q):
            mixed[r : r + 1, h * HEAD_DIM : (h + 1) * HEAD_DIM] = result[h : h + 1, :]
    context_ref[...] = mixed[...].astype(jnp.bfloat16)
    for out in outs:
        out.wait()


def last(plan, parts, pools, page, src, lengths, normed, cosine, sine, query, fresh, wq_new, wkv_new):
    rows = normed.shape[0]
    slots = src.shape[1] * page
    args = [*parts, *pools, src, lengths, normed, cosine, sine, query, fresh, wq_new, wkv_new]
    lead = len(parts) + len(pools)
    return pl.pallas_call(
        functools.partial(last_kernel, plan, len(parts), page),
        out_shape=[
            jax.ShapeDtypeStruct(wq_new.shape, jnp.bfloat16),
            jax.ShapeDtypeStruct(wkv_new.shape, jnp.bfloat16),
            jax.ShapeDtypeStruct((rows, 1, slots, WIDTH), jnp.bfloat16),
            jax.ShapeDtypeStruct(query.shape, jnp.bfloat16),
        ],
        in_specs=[ANY] * len(parts) + [VM, VM, SM, SM, VM, VM, VM, VM, VM, HBM, HBM],
        out_specs=[HBM, HBM, HBM, VM],
        input_output_aliases={lead + 7: 0, lead + 8: 1},
        scratch_shapes=[pltpu.VMEM(part.shape, jnp.bfloat16) for part in parts]
        + [
            pltpu.VMEM((rows, slots, WIDTH), jnp.bfloat16),
            pltpu.VMEM((rows, 8, HEAD_DIM), jnp.float32),
            pltpu.VMEM(query.shape, jnp.float32),
            pltpu.SemaphoreType.DMA((len(parts),)),
            pltpu.SemaphoreType.DMA((len(plan),)),
            pltpu.SemaphoreType.DMA((rows,)),
        ],
        compiler_params=params(LAST_LIMIT),
        cost_estimate=cost(64 << 20, 16 << 20),
    )(*args)


def halves(part, low, rows):
    return [(part, low, 0, rows), (part, low, WIDTH, rows)]


def shards(hidden_state, norm_gain, wq_old, wkv_old, kv_old, page_table, lengths):
    rows = hidden_state.shape[0]
    page = kv_old.shape[2]
    half = wq_old.shape[0] // 2
    rest = wq_old.shape[0] - F
    split = rest // 2

    pairs = []
    for yl in range(2):
        for z in range(4):
            for yh in range(2):
                for x in range(4):
                    here = ((yl * 4 + z) * 2 + yh) * 4 + x
                    pairs.append((here, ((yh * 4 + (z + x) % 4) * 2 + yl) * 4 + x))
    moved = lax.ppermute(wkv_old, ("yl", "z", "yh", "x"), pairs)
    (held,) = pack(([(0, 0, 0, wq_old.shape[0])],), (wq_old,), (moved,), (2 * WIDTH,))
    up = shift(held, "z", 1)
    down = shift(held, "z", -1)
    picked = pick(page_table, kv_old)
    src = picked[2]
    near, far = [
        lax.ppermute(
            picked[flip].reshape(-1, WIDTH),
            ("yl", "yh"),
            [(a * 2 + b, (b ^ flip) * 2 + a) for a in range(2) for b in range(2)],
        )
        for flip in range(2)
    ]
    turned = lax.ppermute(
        moved, ("z", "x"), [(z * 4 + x, z * 4 + (z - x) % 4) for z in range(4) for x in range(4)]
    )

    my_lengths = lax.dynamic_slice_in_dim(lengths, lax.axis_index(SECTION) * rows, rows, 0)
    widened = hidden_state.astype(jnp.float32)
    scale = lax.rsqrt(jnp.mean(widened * widened, axis=1, keepdims=True) + EPSILON)
    normed = (widened * scale * norm_gain[None, :]).astype(jnp.bfloat16)
    spread = HEAD_DIM // 2
    frequency = ROPE_BASE ** (-(jnp.arange(spread, dtype=jnp.float32) * 2.0 / HEAD_DIM))
    angles = my_lengths.astype(jnp.float32)[:, None] * frequency[None, :]
    cosine, sine = jnp.cos(angles), jnp.sin(angles)
    cosine = jnp.concatenate([cosine, cosine], axis=1)
    sine = jnp.concatenate([-sine, sine], axis=1)

    chunk = near.shape[0] // 4
    block = turned.shape[0]
    parts = (up, down, near, far, turned)
    to_up, to_down, to_two, to_across, own = pack(
        (
            halves(0, 0, half) + [(2, chunk, 0, chunk), (3, chunk, 0, chunk), (4, 0, 0, block)],
            halves(1, half, half) + [(2, 3 * chunk, 0, chunk), (3, 3 * chunk, 0, chunk), (4, 0, 0, block)],
            [(2, 2 * chunk, 0, chunk), (3, 2 * chunk, 0, chunk), (4, 0, 0, block)],
            halves(0, 0, F) + halves(1, 0, F) + [(4, 0, 0, block)],
            [(5, 0, 0, 2 * half)],
        ),
        (*parts, wq_old),
        (),
        (WIDTH, WIDTH, WIDTH, WIDTH, 2 * WIDTH),
    )
    across = shift(own, "yl", 1)
    up2 = shift(to_up, "z", 1)
    down2 = shift(to_down, "z", -1)
    two2 = shift(to_two, "z", 2)
    wq_new, query = join(
        (
            (0, 0, 2 * half, "q", 0, 0, 0, 0, 2 * WIDTH),
            (1, 0, 2 * half, "q", 0, -1, 0, 0, 2 * WIDTH),
            (2, 0, 2 * half, "q", 0, 1, 0, 0, 2 * WIDTH),
        ),
        (wq_old, up, down),
        normed,
    )
    across2 = shift(to_across, "yl", 1)

    later = across[F:]
    up3 = shift(later, "z", 1)
    down3 = shift(later, "z", -1)
    page_rows = 2 * half
    wkv_at = page_rows + 2 * chunk
    sorted_pages, to_across3, to_core = sort(
        (near, far, up2, down2, two2, turned, across2),
        [
            (0, 0, 0, 0),
            (1, 0, 0, chunk),
            (2, page_rows, 1, 0),
            (2, page_rows + chunk, 1, chunk),
            (3, page_rows, 3, 0),
            (3, page_rows + chunk, 3, chunk),
            (4, 0, 2, 0),
            (4, chunk, 2, chunk),
        ],
        chunk,
        [
            [(2, 0, F), (2, half, F), (2, wkv_at, block), (3, wkv_at, block), (4, 2 * chunk, block)],
            [
                (5, 0, block),
                (2, wkv_at, block),
                (3, wkv_at, block),
                (4, 2 * chunk, block),
                (6, 4 * F, block),
            ],
        ],
        (across,),
    )
    across3 = shift(to_across3, "yl", 1)
    mine = lax.all_to_all(sorted_pages, "x", split_axis=0, concat_axis=0, tiled=True)
    wq_new, query = join(
        (
            (0, 0, 2 * half, "q", 1, 0, 0, 0, 2 * WIDTH),
            (1, 0, half, "q", 0, 2, 0, 0, WIDTH),
            (1, half, half, "q", 0, 2, 0, WIDTH, WIDTH),
            (2, 0, half, "q", 0, 2, half, 0, WIDTH),
            (2, half, half, "q", 0, 2, half, WIDTH, WIDTH),
            (3, 0, F, "q", 1, -1, 0, 0, WIDTH),
            (3, F, F, "q", 1, -1, 0, WIDTH, WIDTH),
            (3, 2 * F, F, "q", 1, 1, 0, 0, WIDTH),
            (3, 3 * F, F, "q", 1, 1, 0, WIDTH, WIDTH),
        ),
        (across, up2, down2, across2),
        normed,
        (wq_new, query),
    )
    swapped = shift(to_core, "core", 1)

    mine = mine.reshape(-1, WIDTH)
    other = shift(mine, "core", 1)
    swapped2 = shift(across3, "core", 1)
    to_up4, to_down4 = pack(
        ([(0, 0, 0, split)], [(1, split, 0, split)]), (up3, down3), (), (2 * WIDTH, 2 * WIDTH)
    )
    up4 = shift(to_up4, "z", 1)
    down4 = shift(to_down4, "z", -1)
    wq_new, wkv_new, query, fresh = join(
        (
            (0, 0, rest, "q", 1, -1, F, 0, 2 * WIDTH),
            (1, 0, rest, "q", 1, 1, F, 0, 2 * WIDTH),
            (2, 0, F, "q", 1, 2, 0, 0, WIDTH),
            (2, F, F, "q", 1, 2, 0, WIDTH, WIDTH),
            (2, 2 * F, block, "own", 1, -1, 0, 0, WIDTH),
            (2, 2 * F + block, block, "own", 1, 1, 0, 0, WIDTH),
            (2, 2 * F + 2 * block, block, "own", 1, 2, 0, 0, WIDTH),
            (3, 0, block, "own", 0, 0, 0, 0, WIDTH),
            (3, block, block, "own", 0, -1, 0, 0, WIDTH),
            (3, 2 * block, block, "own", 0, 1, 0, 0, WIDTH),
            (3, 3 * block, block, "own", 0, 2, 0, 0, WIDTH),
            (3, 4 * block, block, "own", 1, 0, 0, 0, WIDTH),
        ),
        (up3, down3, across3, to_core),
        normed,
        (wq_new, query),
    )

    spots = ((0, 0), (0, -1), (0, 1), (0, 2), (1, 0))
    spots2 = ((1, -1), (1, 1), (1, 2))
    wq_new, wkv_new, kv_new, context = last(
        (
            *[
                (2, n * block, block, "other", dy, dz, 0, 0, WIDTH)
                for n, (dy, dz) in enumerate(spots)
            ],
            *[
                (3, 2 * F + n * block, block, "other", dy, dz, 0, 0, WIDTH)
                for n, (dy, dz) in enumerate(spots2)
            ],
            (0, 0, split, "q", 1, 2, F, 0, 2 * WIDTH),
            (1, 0, split, "q", 1, 2, F + split, 0, 2 * WIDTH),
        ),
        (up4, down4, swapped, swapped2),
        (mine, other),
        page,
        src,
        lengths,
        normed,
        cosine,
        sine,
        query,
        fresh,
        wq_new,
        wkv_new,
    )
    return (context, kv_new, wq_new, wkv_new)


def solution(mesh):
    torus = Mesh(mesh.devices.reshape(2, 4, 2, 4, 2), ("yl", "z", "yh", "x", "core"))
    return jax.shard_map(
        shards,
        mesh=torus,
        in_specs=(
            P(SECTION, None),
            P(),
            P(SECTION, TENSOR),
            P(TENSOR, SECTION),
            P(SECTION, TENSOR, None, None),
            P(),
            P(),
        ),
        out_specs=(
            P(SECTION, TENSOR),
            P(SECTION, TENSOR, None, None),
            P(None, TENSOR),
            P(None, TENSOR),
        ),
        check_vma=False,
    )
```
